32 devices in a mesh: ctx: 32 (over z, y, x, core), ch: 1.
Axes of the slice: x: 2, y: 2, z: 4, core: 2. Of those that a mesh axis runs over, the one named last changes fastest.
Arguments:
- query_branch: bfloat16 [8192, 2048], P('ctx', 'ch'), may hold values from -6 to 6
- key_branch: bfloat16 [8192, 2048], P('ctx', 'ch'), may hold values from -6 to 6
- value_branch: bfloat16 [8192, 2048], P('ctx', 'ch'), may hold values from -6 to 6
- grad_output: bfloat16 [8192, 2048], P('ctx', 'ch'), may hold values from -6 to 6
- conv_output: bfloat16 [8192, 2048], P('ctx', 'ch'), may hold values from -6 to 6
- filters: float32 [8192, 512], P('ctx'), may hold values from -0.09375 to 0.09375
- genome_blocks: int32 [4], replicated, may hold values from 1 to 16, 32 in all
Outputs:
- grad_query: bfloat16 [8192, 2048], P('ctx', 'ch')
- grad_key: bfloat16 [8192, 2048], P('ctx', 'ch')
- grad_value: bfloat16 [8192, 2048], P('ctx', 'ch')
- grad_filters: float32 [8192, 512], P('ctx', 'ch')
The draws below stay inside these ranges and needn't reach their ends.
Inputs may be any that keep to these rules, and one draw needn't show every extreme that they name: `genome_blocks`: the genomes lie in order and fill the row; the longest covers exactly 16 shards.
All inputs are finite; a program needn't handle non-finite values.
Results may differ from the reference program's by a relative error of at most 0.001.
Values sent between devices are 32-bit elements; how exact they have to be, the bound alone decides.
A program may use at most 128 MiB of HBM per device.

```python
import math
import jax
import jax.numpy as jnp
import numpy as np
from jax import lax

TOK_DEV = 256
CHANNELS = 2048
FILTERS = 512
TOKENS = 8192
MOST = 16
GENOMES = 4
N_CTX = 32


def block_scale(stream_key, extent, pieces, least, top_value):
    factor_of, own = 1.0, jax.random.fold_in(stream_key, 6)
    for dim, parts in pieces:
        draws = jnp.exp(jax.random.uniform(jax.random.fold_in(own, dim), (parts,), jnp.float32, least / len(pieces), top_value / len(pieces)))
        factor_of = factor_of * jnp.repeat(draws, extent[dim] // parts).reshape([-1 if axis == dim else 1 for axis in range(len(extent))])
    return factor_of


def profile(count, total, bound, skew):
    weights = [(1 << 20) // math.isqrt(grade ** skew) + 1 for grade in range(2, count + 1)]
    surplus, given = total - bound - (count - 1), [1] * (count - 1)
    while surplus > 0:
        free = [i for i in range(count - 1) if given[i] < bound]
        mass, left = sum([weights[i] for i in free]), surplus
        for i in free:
            more = min(bound - given[i], max(1, left * weights[i] // mass), surplus)
            given[i] = given[i] + more
            surplus = surplus - more
    return np.array([bound] + given)


def ragged(stream_key, number_of, total, bound, skew):
    if number_of == 2:
        one = jax.random.randint(stream_key, (), max(1, total - bound), min(bound, total - 1) + 1)
        return jnp.stack([one, total - one])
    tallies = jnp.asarray(profile(number_of, total, bound, skew), jnp.int32)
    twos = (number_of - 1) // 2
    giver, sink = tallies[1:1 + 2 * twos:2], tallies[2:2 + 2 * twos:2]
    slack = jnp.minimum(giver - 1, bound - sink)
    shifted = jax.random.randint(jax.random.fold_in(stream_key, 1), (twos,), 0, 1 << 20) % (slack + 1)
    tallies = tallies.at[1:1 + 2 * twos:2].set(giver - shifted).at[2:2 + 2 * twos:2].set(sink + shifted)
    return tallies[jax.random.permutation(jax.random.fold_in(stream_key, 2), number_of)]


def bell_draw(rng, extent, deviation, most, pieces=(), dtype=jnp.bfloat16):
    loudness = block_scale(rng, extent, pieces, -0.22, 0.18) if pieces else 1.0
    values = jax.random.normal(rng, extent, jnp.float32) * deviation * loudness
    return jnp.minimum(jnp.maximum(values, -most), most).astype(dtype)


def setup_inputs(seed: int = 0) -> dict:
    key_of = jax.random.split(jax.random.key(seed), 8)
    return {
        "query_branch": bell_draw(key_of[0], (TOKENS, CHANNELS), 1.0, 6.0, ((0, 32),)),
        "key_branch": bell_draw(key_of[1], (TOKENS, CHANNELS), 1.0, 6.0, ((0, 32),)),
        "value_branch": bell_draw(key_of[2], (TOKENS, CHANNELS), 1.0, 6.0, ((0, 32),)),
        "grad_output": bell_draw(key_of[3], (TOKENS, CHANNELS), 1.0, 6.0, ((0, 32),)),
        "conv_output": bell_draw(key_of[4], (TOKENS, CHANNELS), 1.0, 6.0, ((0, 32),)),
        "filters": bell_draw(key_of[5], (TOKENS, FILTERS), (MOST * TOK_DEV) ** -0.5, 0.09375, ((0, 32),), jnp.float32),
        "genome_blocks": ragged(key_of[6], GENOMES, N_CTX, MOST, 2).astype(jnp.int32),
    }


def reference(query_branch, key_branch, value_branch, grad_output, conv_output, filters, genome_blocks):
    length, channels = query_branch.shape
    repeats = channels // filters.shape[1]
    query32 = query_branch.astype(jnp.float32)
    key32 = key_branch.astype(jnp.float32)
    gated = query32 * key32
    carried = grad_output.astype(jnp.float32) * value_branch.astype(jnp.float32)
    grad_value = (grad_output.astype(jnp.float32) * conv_output.astype(jnp.float32)).astype(jnp.bfloat16)
    ends = (jnp.cumsum(genome_blocks) * TOK_DEV).astype(jnp.int32)
    places = jnp.arange(length).astype(jnp.int32)
    owners = jnp.sum((ends[None, :] <= places[:, None]).astype(jnp.int32), axis=1)
    full_len = 2 * length
    filter_spec = jnp.tile(jnp.conj(jnp.fft.rfft(filters, n=full_len, axis=0)), (1, repeats))

    def one_genome(state, genome):
        back, lag_sum = state
        inside = (owners == genome).astype(jnp.float32)[:, None]
        carried_spec = jnp.fft.rfft(carried * inside, n=full_len, axis=0)
        gated_spec = jnp.fft.rfft(gated * inside, n=full_len, axis=0)
        back = back + jnp.fft.irfft(carried_spec * filter_spec, n=full_len, axis=0)[:length] * inside
        cross = jnp.fft.irfft(carried_spec * jnp.conj(gated_spec), n=full_len, axis=0)[:length]
        lag_sum = lag_sum + cross.reshape(length, repeats, -1).sum(axis=1)
        return (back, lag_sum), None

    start = (jnp.zeros((length, channels), jnp.float32), jnp.zeros(filters.shape, jnp.float32))
    (back, lag_sum), _ = lax.scan(one_genome, start, jnp.arange(GENOMES).astype(jnp.int32))
    grad_query = (back * key32).astype(jnp.bfloat16)
    grad_key = (back * query32).astype(jnp.bfloat16)
    grad_filters = lag_sum * (TOKENS ** -0.5)
    return grad_query, grad_key, grad_value, grad_filters
```

```python
import functools

import jax
import jax.numpy as jnp
from jax import lax
from jax.experimental import pallas as pl
from jax.experimental.pallas import tpu as pltpu
from jax.sharding import PartitionSpec as P

HALF = 128
GROUP = 8
PIECES = 2
NT = (((1,), (1,)), ((), ()))


def split_bf16(x):
    high = x.astype(jnp.bfloat16)
    low = (x - high.astype(jnp.float32)).astype(jnp.bfloat16)
    return high, low


def conv_kernel(
    ids_ref, ids_odd_ref, carried_ref, gated_ref, filter_ref,
    back_ref, lags_ref,
    even, odd, weights, accum, low_sum, high_sum,
):
    n = carried_ref.shape[0]
    rows = GROUP * n
    pairs = filter_ref.shape[1]
    lane = lax.broadcasted_iota(jnp.int32, (HALF, HALF), 1)
    place = lax.broadcasted_iota(jnp.int32, (HALF, HALF), 0)

    carried = carried_ref[:, 0]
    even[: rows] = carried.reshape(rows, HALF)
    even[rows:] = jnp.zeros((even.shape[0] - rows, HALF), jnp.float32)
    odd[...] = jnp.zeros_like(odd)
    odd[: rows - 4] = even[4:rows]

    def build(c, before):
        for side in range(2):
            row = filter_ref[0, c, :, side * HALF:(side + 1) * HALF]
            turned = pltpu.roll(
                jnp.broadcast_to(row, (HALF, HALF)), 0, 1, stride=1, stride_axis=0
            )
            tile = jnp.where(lane >= place, turned, before)
            high, low = split_bf16(tile)
            weights[c, :HALF, side * HALF:(side + 1) * HALF] = high
            weights[c, HALF:, side * HALF:(side + 1) * HALF] = low
            before = turned
        return before

    lax.fori_loop(0, pairs, build, jnp.zeros((HALF, HALF), jnp.float32))

    swap = (lane + place == HALF - 1).astype(jnp.bfloat16)
    gated_high, gated_low = split_bf16(gated_ref[:, 0].reshape(rows, HALF))
    turned_high = lax.dot_general(
        swap, gated_high, NT, preferred_element_type=jnp.float32
    ).astype(jnp.bfloat16)
    turned_low = lax.dot_general(
        swap, gated_low, NT, preferred_element_type=jnp.float32
    ).astype(jnp.bfloat16)

    accum[...] = jnp.zeros_like(accum)

    def lag_pair(c, _):
        start = pl.multiple_of(c * GROUP, GROUP)
        own = ids_ref[:rows]
        later = jnp.concatenate(
            [
                jnp.where(ids_ref[pl.ds(start, rows)] == own, even[pl.ds(start, rows)], 0.0),
                jnp.where(ids_odd_ref[pl.ds(start, rows)] == own, odd[pl.ds(start, rows)], 0.0),
            ],
            axis=1,
        )
        high, low = split_bf16(later)
        accum[...] += lax.dot_general(high, weights[c], NT, preferred_element_type=jnp.float32)
        accum[:, :HALF] += lax.dot_general(
            low, weights[c, :HALF], NT, preferred_element_type=jnp.float32
        )
        outer = (
            jnp.dot(turned_high, high, preferred_element_type=jnp.float32)
            + jnp.dot(turned_low, high, preferred_element_type=jnp.float32)
            + jnp.dot(turned_high, low, preferred_element_type=jnp.float32)
        )
        for side in range(2):
            turned = pltpu.roll(
                outer[:, side * HALF:(side + 1) * HALF], 1, 1, stride=1, stride_axis=0
            )
            inside = lane <= place
            here = jnp.where(inside, turned, 0.0).reshape(HALF // GROUP, GROUP, HALF)
            prior = jnp.where(inside, 0.0, turned).reshape(HALF // GROUP, GROUP, HALF)
            high_sum[2 * c + side] = jnp.sum(here, axis=0)
            low_sum[2 * c + side] = jnp.sum(prior, axis=0)
        return 0

    low_sum[2 * pairs] = jnp.zeros((GROUP, HALF), jnp.float32)
    lax.fori_loop(0, pairs, lag_pair, 0)
    total = accum[:, :HALF] + accum[:, HALF:]
    back_ref[:, 0] = total.reshape(n, GROUP, HALF)
    lags_ref[0] = jnp.sum(high_sum[...] + low_sum[1:], axis=1)


def convolve(ids, ids_odd, carried, gated, filters):
    n, width = carried.shape[:2]
    pairs = filters.shape[1]
    rows = GROUP * n
    padded = ids.shape[0]
    whole = pl.BlockSpec((padded, HALF), lambda f: (0, 0))
    signal = pl.BlockSpec((n, 1, GROUP, HALF), lambda f: (0, f, 0, 0))
    flops = width * 2 * pairs * 2 * rows * 256 * (256 + 128 + 192)
    return pl.pallas_call(
        conv_kernel,
        grid=(width,),
        in_specs=[
            whole, whole, signal, signal,
            pl.BlockSpec((1, pairs, 1, 2 * HALF), lambda f: (f, 0, 0, 0)),
        ],
        out_specs=[signal, pl.BlockSpec((1, 2 * pairs, HALF), lambda f: (f, 0, 0))],
        out_shape=[
            jax.ShapeDtypeStruct(carried.shape, jnp.float32),
            jax.ShapeDtypeStruct((width, 2 * pairs, HALF), jnp.float32),
        ],
        scratch_shapes=[
            pltpu.VMEM((padded, HALF), jnp.float32),
            pltpu.VMEM((padded, HALF), jnp.float32),
            pltpu.VMEM((pairs, 256, 256), jnp.bfloat16),
            pltpu.VMEM((rows, 256), jnp.float32),
            pltpu.VMEM((2 * pairs + 1, GROUP, HALF), jnp.float32),
            pltpu.VMEM((2 * pairs, GROUP, HALF), jnp.float32),
        ],
        compiler_params=pltpu.CompilerParams(vmem_limit_bytes=32 * 1024 * 1024),
        cost_estimate=pl.CostEstimate(
            flops=flops, bytes_accessed=3 * carried.size * 4, transcendentals=0
        ),
    )(ids, ids_odd, carried, gated, filters)


def local(query_branch, key_branch, value_branch, grad_output, conv_output, filters, genome_blocks):
    rows, channels = query_branch.shape
    width = filters.shape[1]
    repeats = channels // width
    blocks = lax.axis_size("ctx")
    pairs = blocks // 2
    own = width // blocks
    part = own // PIECES
    query32 = query_branch.astype(jnp.float32)
    key32 = key_branch.astype(jnp.float32)
    gated = query32 * key32
    carried = grad_output.astype(jnp.float32) * value_branch.astype(jnp.float32)
    grad_value = (grad_output.astype(jnp.float32) * conv_output.astype(jnp.float32)).astype(
        jnp.bfloat16
    )
    ends = jnp.cumsum(genome_blocks)
    block_ids = jnp.sum(
        (ends[None, :] <= jnp.arange(blocks, dtype=jnp.int32)[:, None]).astype(jnp.int32), axis=1
    )
    row_ids = jnp.repeat(block_ids, GROUP)
    pad = jnp.full((GROUP * pairs,), -1, jnp.int32)
    row_ids = jnp.concatenate([row_ids, pad])
    odd_ids = jnp.concatenate([row_ids[4:], pad[:4]])
    ids = jnp.broadcast_to(row_ids[:, None], (row_ids.shape[0], HALF))
    ids_odd = jnp.broadcast_to(odd_ids[:, None], ids.shape)

    def spread(signal):
        parts = signal.reshape(2, HALF, repeats, blocks, own).transpose(3, 4, 0, 2, 1)
        if repeats < 4:
            parts = jnp.pad(parts, ((0, 0), (0, 0), (0, 0), (0, 4 - repeats), (0, 0)))
        return parts.reshape(blocks, own, GROUP, HALF)

    def exchange(x):
        return lax.all_to_all(x, "ctx", split_axis=0, concat_axis=0, tiled=True)

    gated_parts = spread(gated)
    carried_parts = spread(carried)
    filter_parts = filters.reshape(rows, blocks, own).transpose(1, 2, 0)
    own_filters = exchange(filter_parts)[:pairs].transpose(1, 0, 2)
    backs, lags = [], []
    for piece in range(PIECES):
        chosen = slice(piece * part, (piece + 1) * part)
        back, lag = convolve(
            ids, ids_odd, exchange(carried_parts[:, chosen]), exchange(gated_parts[:, chosen]),
            own_filters[chosen, :, None],
        )
        backs.append(exchange(back))
        lags.append(lag)
    lag = jnp.concatenate(lags, axis=0).reshape(own, pairs, rows).transpose(1, 0, 2)
    lag = exchange(jnp.concatenate([lag, jnp.zeros_like(lag)], axis=0))
    back = jnp.concatenate(backs, axis=1).reshape(blocks, own, 2, 4, HALF)[:, :, :, :repeats]
    back = back.transpose(2, 4, 3, 0, 1).reshape(rows, channels)
    scaled = lag.transpose(2, 0, 1).reshape(rows, width) * (rows * blocks) ** (-0.5)
    grad_query = (back * key32).astype(jnp.bfloat16)
    grad_key = (back * query32).astype(jnp.bfloat16)
    grad_filters = lax.psum_scatter(scaled, "ch", scatter_dimension=1, tiled=True)
    return (grad_query, grad_key, grad_value, grad_filters)


def solution(mesh):
    in_specs = (
        P("ctx", "ch"),
        P("ctx", "ch"),
        P("ctx", "ch"),
        P("ctx", "ch"),
        P("ctx", "ch"),
        P("ctx", None),
        P(),
    )
    out_specs = (P("ctx", "ch"), P("ctx", "ch"), P("ctx", "ch"), P("ctx", "ch"))
    return jax.shard_map(local, mesh=mesh, in_specs=in_specs, out_specs=out_specs, check_vma=False)
```

```python
import jax
import jax.numpy as jnp
from jax import lax
from jax.experimental import pallas as pl
from jax.experimental.pallas import tpu as pltpu
from jax.sharding import PartitionSpec as P

HALF = 128
GROUP = 8
PART = 2
UNROLL = 4
NT = (((1,), (1,)), ((), ()))


def split_bf16(x):
    high = x.astype(jnp.bfloat16)
    low = (x - high.astype(jnp.float32)).astype(jnp.bfloat16)
    return high, low


def conv_one(
    f, ids_ref, ids_odd_ref, recv, filter_in, back_out, lag_out,
    even, odd, weights, accum, low_sum, high_sum,
):
    n = recv.shape[0]
    rows = GROUP * n
    pairs = filter_in.shape[0]
    lane = lax.broadcasted_iota(jnp.int32, (HALF, HALF), 1)
    place = lax.broadcasted_iota(jnp.int32, (HALF, HALF), 0)

    carried = recv[:, f, 0].reshape(rows, HALF)
    even[:rows] = carried
    odd[: rows - 4] = even[4:rows]

    def build(c, before):
        for pair in range(UNROLL):
            for side in range(2):
                row = filter_in[c * UNROLL + pair, f, side]
                turned = pltpu.roll(
                    jnp.broadcast_to(row, (HALF, HALF)), 0, 1, stride=1, stride_axis=0
                )
                tile = jnp.where(lane >= place, turned, before)
                high, low = split_bf16(tile)
                at = pair * 2 * HALF + side * HALF
                weights[c, :HALF, at:at + HALF] = high
                weights[c, HALF:, at:at + HALF] = low
                before = turned
        return before

    lax.fori_loop(0, pairs // UNROLL, build, jnp.zeros((HALF, HALF), jnp.float32))

    swap = (lane + place == HALF - 1).astype(jnp.bfloat16)
    gated_high, gated_low = split_bf16(recv[:, f, 1].reshape(rows, HALF))
    turned_high = lax.dot_general(
        swap, gated_high, NT, preferred_element_type=jnp.float32
    ).astype(jnp.bfloat16)
    turned_low = lax.dot_general(
        swap, gated_low, NT, preferred_element_type=jnp.float32
    ).astype(jnp.bfloat16)
    turned_both = jnp.concatenate([turned_high, turned_low], axis=0)

    accum[...] = jnp.zeros_like(accum)

    def lag_group(c, _):
        own = ids_ref[:rows]
        later = []
        for pair in range(UNROLL):
            start = pl.multiple_of((c * UNROLL + pair) * GROUP, GROUP)
            for ids, source in ((ids_ref, even), (ids_odd_ref, odd)):
                later.append(
                    jnp.where(ids[pl.ds(start, rows)] == own, source[pl.ds(start, rows)], 0.0)
                )
        high, low = split_bf16(jnp.concatenate(later, axis=1))
        accum[...] += lax.dot_general(high, weights[c], NT, preferred_element_type=jnp.float32)
        accum[:, :HALF] += lax.dot_general(
            low, weights[c, :HALF], NT, preferred_element_type=jnp.float32
        )
        both = jnp.dot(turned_both, high, preferred_element_type=jnp.float32)
        outer = (
            both[:HALF] + both[HALF:] + jnp.dot(turned_high, low, preferred_element_type=jnp.float32)
        )
        inside = lane <= place
        for side in range(2 * UNROLL):
            turned = pltpu.roll(
                outer[:, side * HALF:(side + 1) * HALF], 1, 1, stride=1, stride_axis=0
            )
            here = jnp.where(inside, turned, 0.0).reshape(HALF // GROUP, GROUP, HALF)
            prior = jnp.where(inside, 0.0, turned).reshape(HALF // GROUP, GROUP, HALF)
            high_sum[2 * UNROLL * c + side] = jnp.sum(here, axis=0)
            low_sum[2 * UNROLL * c + side] = jnp.sum(prior, axis=0)
        return 0

    lax.fori_loop(0, pairs // UNROLL, lag_group, 0)
    total = accum[:, :HALF] + accum[:, HALF:]
    back_out[:, f] = total.reshape(n, GROUP, HALF)
    lags = jnp.sum(high_sum[...] + low_sum[1:], axis=1, keepdims=True)
    lag_out[:, :, f] = lags.reshape(pairs, 2, 1, HALF)


def fused_kernel(
    ids_ref, ids_odd_ref, send, filter_send,
    back_in, lag_in,
    recv, filter_in, back_out, lag_out,
    even, odd, weights, accum, low_sum, high_sum,
    filter_sems, lag_sems, out_sems, in_sems, back_out_sems, back_in_sems,
):
    n, own = send.shape[:2]
    pairs = filter_in.shape[0]
    pieces = own // PART
    me = lax.axis_index("ctx")

    def partner(i):
        return lax.rem(me + i, n)

    def copy(source, target, send_sem, recv_sem, device):
        return pltpu.make_async_remote_copy(
            src_ref=source, dst_ref=target, send_sem=send_sem, recv_sem=recv_sem,
            device_id={"ctx": device}, device_id_type=pl.DeviceIdType.MESH,
        )

    def each_partner(act):
        def step(i, _):
            act(partner(i))
            return 0

        lax.fori_loop(1, n, step, 0)

    def chosen(piece):
        return pl.ds(piece * PART, PART)

    def waiter(ref, send_sem, recv_sem):
        return copy(ref, ref, send_sem, recv_sem, partner(1))

    barrier = pltpu.get_barrier_semaphore()
    each_partner(
        lambda other: pl.semaphore_signal(
            barrier, inc=1, device_id={"ctx": other}, device_id_type=pl.DeviceIdType.MESH
        )
    )
    pl.semaphore_wait(barrier, n - 1)

    @pl.when(me < pairs)
    def _():
        each_partner(
            lambda other: copy(
                filter_send.at[other], filter_in.at[me], filter_sems.at[0], filter_sems.at[1], other
            ).start()
        )

    def send_piece(piece, _):
        each_partner(
            lambda other: copy(
                send.at[other, chosen(piece)], recv.at[me, chosen(piece)],
                out_sems.at[piece], in_sems.at[piece], other,
            ).start()
        )
        return 0

    lax.fori_loop(0, pieces, send_piece, 0)

    recv[me] = send[me]
    even[...] = jnp.zeros_like(even)
    odd[...] = jnp.zeros_like(odd)
    low_sum[2 * pairs] = jnp.zeros((GROUP, HALF), jnp.float32)

    @pl.when(me < pairs)
    def _():
        filter_in[me] = filter_send[me]
        waiter(filter_in.at[pl.ds(0, pairs - 1)], filter_sems.at[0], filter_sems.at[1]).wait_recv()

    @pl.when(me >= pairs)
    def _():
        waiter(filter_in, filter_sems.at[0], filter_sems.at[1]).wait_recv()

    def work(piece, _):
        waiter(
            recv.at[pl.ds(0, n - 1), chosen(piece)], out_sems.at[piece], in_sems.at[piece]
        ).wait_recv()

        def one(i, _):
            conv_one(
                piece * PART + i, ids_ref, ids_odd_ref, recv, filter_in, back_out, lag_out,
                even, odd, weights, accum, low_sum, high_sum,
            )
            return 0

        lax.fori_loop(0, PART, one, 0)
        each_partner(
            lambda other: copy(
                back_out.at[other, chosen(piece)], back_in.at[me, chosen(piece)],
                back_out_sems.at[piece], back_in_sems.at[piece], other,
            ).start()
        )
        back_in[me, chosen(piece)] = back_out[me, chosen(piece)]
        return 0

    lax.fori_loop(0, pieces, work, 0)

    def send_lags(other, _):
        @pl.when(other != me)
        def _():
            copy(
                lag_out.at[other], lag_in.at[me], lag_sems.at[0], lag_sems.at[1], other
            ).start()

        return 0

    lax.fori_loop(0, pairs, send_lags, 0)

    @pl.when(me < pairs)
    def _():
        lag_in[me] = lag_out[me]
        waiter(filter_send.at[pl.ds(0, n - 1)], filter_sems.at[0], filter_sems.at[1]).wait_send()
        waiter(lag_out.at[pl.ds(0, pairs - 1)], lag_sems.at[0], lag_sems.at[1]).wait_send()
        waiter(lag_in.at[pl.ds(0, n - 1)], lag_sems.at[0], lag_sems.at[1]).wait_recv()

    @pl.when(me >= pairs)
    def _():
        lag_in[...] = jnp.zeros_like(lag_in)
        waiter(lag_out, lag_sems.at[0], lag_sems.at[1]).wait_send()

    def finish(piece, _):
        waiter(
            send.at[pl.ds(0, n - 1), chosen(piece)], out_sems.at[piece], in_sems.at[piece]
        ).wait_send()
        waiter(
            back_in.at[pl.ds(0, n - 1), chosen(piece)], back_out_sems.at[piece],
            back_in_sems.at[piece],
        ).wait()
        return 0

    lax.fori_loop(0, pieces, finish, 0)


def convolve(ids, ids_odd, signals, filters):
    n, own = signals.shape[:2]
    pairs = n // 2
    pieces = own // PART
    rows = GROUP * n
    padded = ids.shape[0]
    vmem = pl.BlockSpec(memory_space=pltpu.VMEM)
    flops = own * 2 * pairs * 2 * rows * 256 * (256 + 128 + 192)
    return pl.pallas_call(
        fused_kernel,
        in_specs=[vmem] * 4,
        out_specs=[vmem] * 2,
        out_shape=[
            jax.ShapeDtypeStruct((n, own, GROUP, HALF), jnp.float32),
            jax.ShapeDtypeStruct((n, 2, own, 1, HALF), jnp.float32),
        ],
        scratch_shapes=[
            pltpu.VMEM(signals.shape, jnp.float32),
            pltpu.VMEM((pairs, own, 2, 1, HALF), jnp.float32),
            pltpu.VMEM((n, own, GROUP, HALF), jnp.float32),
            pltpu.VMEM((pairs, 2, own, 1, HALF), jnp.float32),
            pltpu.VMEM((padded, HALF), jnp.float32),
            pltpu.VMEM((padded, HALF), jnp.float32),
            pltpu.VMEM((pairs // UNROLL, 256, 256 * UNROLL), jnp.bfloat16),
            pltpu.VMEM((rows, 256), jnp.float32),
            pltpu.VMEM((2 * pairs + 1, GROUP, HALF), jnp.float32),
            pltpu.VMEM((2 * pairs, GROUP, HALF), jnp.float32),
            pltpu.SemaphoreType.DMA((2,)),
            pltpu.SemaphoreType.DMA((2,)),
            pltpu.SemaphoreType.DMA((pieces,)),
            pltpu.SemaphoreType.DMA((pieces,)),
            pltpu.SemaphoreType.DMA((pieces,)),
            pltpu.SemaphoreType.DMA((pieces,)),
        ],
        compiler_params=pltpu.CompilerParams(
            collective_id=0, has_side_effects=True, vmem_limit_bytes=48 * 1024 * 1024
        ),
        cost_estimate=pl.CostEstimate(
            flops=flops, bytes_accessed=3 * signals.size * 4, transcendentals=0
        ),
    )(ids, ids_odd, signals, filters)


def local(query_branch, key_branch, value_branch, grad_output, conv_output, filters, genome_blocks):
    rows, channels = query_branch.shape
    width = filters.shape[1]
    repeats = channels // width
    blocks = lax.axis_size("ctx")
    pairs = blocks // 2
    own = width // blocks
    query32 = query_branch.astype(jnp.float32)
    key32 = key_branch.astype(jnp.float32)
    gated = query32 * key32
    carried = grad_output.astype(jnp.float32) * value_branch.astype(jnp.float32)
    grad_value = (grad_output.astype(jnp.float32) * conv_output.astype(jnp.float32)).astype(
        jnp.bfloat16
    )
    ends = jnp.cumsum(genome_blocks)
    block_ids = jnp.sum(
        (ends[None, :] <= jnp.arange(blocks, dtype=jnp.int32)[:, None]).astype(jnp.int32), axis=1
    )
    row_ids = jnp.repeat(block_ids, GROUP)
    pad = jnp.full((GROUP * pairs,), -1, jnp.int32)
    row_ids = jnp.concatenate([row_ids, pad])
    odd_ids = jnp.concatenate([row_ids[4:], pad[:4]])
    ids = jnp.broadcast_to(row_ids[:, None], (row_ids.shape[0], HALF))
    ids_odd = jnp.broadcast_to(odd_ids[:, None], ids.shape)

    def spread(signal):
        parts = signal.reshape(2, HALF, repeats, blocks, own).transpose(3, 4, 0, 2, 1)
        if repeats < 4:
            parts = jnp.pad(parts, ((0, 0), (0, 0), (0, 0), (0, 4 - repeats), (0, 0)))
        return parts.reshape(blocks, own, GROUP, HALF)

    signals = jnp.stack([spread(carried), spread(gated)], axis=2)
    filter_parts = filters.reshape(2, HALF, blocks, own).transpose(2, 3, 0, 1)
    back, lag = convolve(ids, ids_odd, signals, filter_parts[:, :, :, None])
    back = back.reshape(blocks, own, 2, 4, HALF)[:, :, :, :repeats]
    back = back.transpose(2, 4, 3, 0, 1).reshape(rows, channels)
    lag = lag[:, :, :, 0].transpose(1, 3, 0, 2).reshape(rows, width)
    scaled = lag * (rows * blocks) ** (-0.5)
    grad_query = (back * key32).astype(jnp.bfloat16)
    grad_key = (back * query32).astype(jnp.bfloat16)
    grad_filters = lax.psum_scatter(scaled, "ch", scatter_dimension=1, tiled=True)
    return (grad_query, grad_key, grad_value, grad_filters)


def solution(mesh):
    in_specs = (
        P("ctx", "ch"),
        P("ctx", "ch"),
        P("ctx", "ch"),
        P("ctx", "ch"),
        P("ctx", "ch"),
        P("ctx", None),
        P(),
    )
    out_specs = (P("ctx", "ch"), P("ctx", "ch"), P("ctx", "ch"), P("ctx", "ch"))
    return jax.shard_map(local, mesh=mesh, in_specs=in_specs, out_specs=out_specs, check_vma=False)
```

```python
import functools

import jax
import jax.numpy as jnp
from jax import lax
from jax.experimental import pallas as pl
from jax.experimental.pallas import tpu as pltpu
from jax.sharding import PartitionSpec as P

HALF = 128
GROUP = 8
PART = 2
UNROLL = 4
NT = (((1,), (1,)), ((), ()))


def split_bf16(x):
    high = x.astype(jnp.bfloat16)
    low = (x - high.astype(jnp.float32)).astype(jnp.bfloat16)
    return high, low


def make_masks(genomes, masks):
    lags, rows = masks.shape[:2]
    row = lax.broadcasted_iota(jnp.int32, (rows, HALF), 0)

    def owner(place):
        block = lax.shift_right_logical(place, 3)
        found = jnp.zeros((rows, HALF), jnp.int32)
        end = 0
        for g in range(genomes.shape[0]):
            end = end + genomes[g]
            found = found + jnp.where(block >= end, 1, 0)
        return found

    own = owner(row)

    def one(lag, _):
        same = owner(row + 4 * lag) == own
        masks[lag] = jnp.where(same, 1.0, 0.0).astype(jnp.bfloat16)
        return 0

    lax.fori_loop(0, lags, one, 0)


def conv_one(
    f, masks, recv, filter_in, back_out, lag_out,
    base, shift_high, shift_low, weights, accum, low_sum, high_sum,
):
    n = recv.shape[0]
    rows = GROUP * n
    pairs = filter_in.shape[0]
    lane = lax.broadcasted_iota(jnp.int32, (GROUP, HALF), 1)
    place = lax.broadcasted_iota(jnp.int32, (GROUP, HALF), 0)

    base[:rows] = recv[:, f, 0].reshape(rows, HALF)
    for move in range(4):
        high, low = split_bf16(base[4 * move:4 * move + rows])
        shift_high[move, :rows] = high
        shift_low[move, :rows] = low

    def build(c, before):
        for pair in range(UNROLL):
            for side in range(2):
                row = filter_in[c * UNROLL + pair, f, side]
                first = pltpu.roll(
                    jnp.broadcast_to(row, (GROUP, HALF)), 1, 1, stride=1, stride_axis=0
                )
                turned = [first] + [
                    pltpu.roll(first, GROUP * p, 1) for p in range(1, HALF // GROUP)
                ]
                tile = jnp.concatenate(
                    [
                        jnp.where(lane <= place + GROUP * p, turned[p], before[p])
                        for p in range(HALF // GROUP)
                    ],
                    axis=0,
                )
                high, low = split_bf16(tile)
                at = pair * 2 * HALF + side * HALF
                weights[c, at:at + HALF, :HALF] = high
                weights[c, at:at + HALF, HALF:] = low
                before = turned
        return before

    lax.fori_loop(
        0, pairs // UNROLL, build, [jnp.zeros((GROUP, HALF), jnp.float32)] * (HALF // GROUP)
    )

    swap = (
        lax.broadcasted_iota(jnp.int32, (HALF, HALF), 1)
        + lax.broadcasted_iota(jnp.int32, (HALF, HALF), 0)
        == HALF - 1
    ).astype(jnp.bfloat16)
    gated_high, gated_low = split_bf16(recv[:, f, 1].reshape(rows, HALF))
    turned_high = lax.dot_general(
        swap, gated_high, NT, preferred_element_type=jnp.float32
    ).astype(jnp.bfloat16)
    turned_low = lax.dot_general(
        swap, gated_low, NT, preferred_element_type=jnp.float32
    ).astype(jnp.bfloat16)
    turned_both = jnp.concatenate([turned_high, turned_low], axis=0)

    accum[...] = jnp.zeros_like(accum)

    def lag_group(c, _):
        highs, lows = [], []
        for e in range(2 * UNROLL):
            lag = 2 * UNROLL * c + e
            window = pl.ds(pl.multiple_of((2 * UNROLL * c + e - e % 4) * 4, 16), rows)
            mask = masks[lag]
            highs.append(shift_high[e % 4, window] * mask)
            lows.append(shift_low[e % 4, window] * mask)
        high = jnp.concatenate(highs, axis=1)
        low = jnp.concatenate(lows, axis=1)
        accum[...] += jnp.dot(high, weights[c], preferred_element_type=jnp.float32)
        accum[:, :HALF] += jnp.dot(
            low, weights[c, :, :HALF], preferred_element_type=jnp.float32
        )
        both = jnp.dot(turned_both, high, preferred_element_type=jnp.float32)
        outer = (
            both[:HALF] + both[HALF:] + jnp.dot(turned_high, low, preferred_element_type=jnp.float32)
        )
        for side in range(2 * UNROLL):
            here = jnp.zeros((GROUP, HALF), jnp.float32)
            prior = jnp.zeros((GROUP, HALF), jnp.float32)
            for p in range(HALF // GROUP):
                part = outer[GROUP * p:GROUP * p + GROUP, side * HALF:(side + 1) * HALF]
                part = pltpu.roll(part, GROUP * p + 1, 1)
                inside = lane <= GROUP * p
                here = here + jnp.where(inside, part, 0.0)
                prior = prior + jnp.where(inside, 0.0, part)
            here = pltpu.roll(here, 0, 1, stride=1, stride_axis=0)
            prior = pltpu.roll(prior, 0, 1, stride=1, stride_axis=0)
            wrapped = lane < place
            high_sum[2 * UNROLL * c + side] = here + jnp.where(wrapped, prior, 0.0)
            low_sum[2 * UNROLL * c + side] = jnp.where(wrapped, 0.0, prior)
        return 0

    lax.fori_loop(0, pairs // UNROLL, lag_group, 0)
    total = accum[:, :HALF] + accum[:, HALF:]
    back_out[:, f] = total.reshape(n, GROUP, HALF)
    lags = jnp.sum(high_sum[...] + low_sum[1:], axis=1, keepdims=True)
    lag_out[:, :, f] = lags.reshape(pairs, 2, 1, HALF)


def spread_product(first, second, sig, send_rows, repeats):
    channels = first.shape[1]
    width = channels // repeats
    for half in range(2):
        for start in range(0, channels, HALF):
            at = (slice(half * HALF, (half + 1) * HALF), slice(start, start + HALF))
            product = first[at].astype(jnp.float32) * second[at].astype(jnp.float32)
            turn, column = start // width, start % width
            row = column * 2 * GROUP + sig * GROUP + half * 4 + turn
            send_rows[pl.ds(row, HALF, stride=2 * GROUP)] = product.T


def fused_kernel(
    repeats, genomes, query, key, value, grad, filter_send,
    back_in, lag_in,
    send, recv, filter_in, back_out, lag_out,
    masks, base, shift_high, shift_low, weights, accum, low_sum, high_sum,
    filter_sems, lag_sems, out_sems, in_sems, back_out_sems, back_in_sems,
):
    n, own = filter_send.shape[:2]
    pairs = filter_in.shape[0]
    pieces = own // PART
    me = lax.axis_index("ctx")

    def partner(i):
        return lax.rem(me + i, n)

    def copy(source, target, send_sem, recv_sem, device):
        return pltpu.make_async_remote_copy(
            src_ref=source, dst_ref=target, send_sem=send_sem, recv_sem=recv_sem,
            device_id={"ctx": device}, device_id_type=pl.DeviceIdType.MESH,
        )

    def each_partner(act):
        def step(i, _):
            act(partner(i))
            return 0

        lax.fori_loop(1, n, step, 0)

    def chosen(piece):
        return pl.ds(piece * PART, PART)

    def sent(other, piece):
        count = PART * 2 * GROUP
        start = pl.multiple_of(other * (own * 2 * GROUP) + piece * count, count)
        return send_blocks(start, count)

    def send_blocks(start, count):
        return send.at[pl.ds(start, count)].reshape(count // 16, 2, GROUP, HALF)

    def waiter(ref, send_sem, recv_sem):
        return copy(ref, ref, send_sem, recv_sem, partner(1))

    barrier = pltpu.get_barrier_semaphore()
    each_partner(
        lambda other: pl.semaphore_signal(
            barrier, inc=1, device_id={"ctx": other}, device_id_type=pl.DeviceIdType.MESH
        )
    )
    if repeats < 4:
        send[...] = jnp.zeros_like(send)
    spread_product(grad, value, 0, send, repeats)
    spread_product(query, key, 1, send, repeats)
    pl.semaphore_wait(barrier, n - 1)

    @pl.when(me < pairs)
    def _():
        each_partner(
            lambda other: copy(
                filter_send.at[other], filter_in.at[me], filter_sems.at[0], filter_sems.at[1], other
            ).start()
        )

    def send_piece(piece, _):
        each_partner(
            lambda other: copy(
                sent(other, piece), recv.at[me, chosen(piece)],
                out_sems.at[piece], in_sems.at[piece], other,
            ).start()
        )
        return 0

    lax.fori_loop(0, pieces, send_piece, 0)

    mine = send[pl.ds(pl.multiple_of(me * (own * 2 * GROUP), 16), own * 2 * GROUP)]
    recv[me] = mine.reshape(own, 2, GROUP, HALF)
    make_masks(genomes, masks)
    base[...] = jnp.zeros_like(base)
    shift_high[...] = jnp.zeros_like(shift_high)
    shift_low[...] = jnp.zeros_like(shift_low)
    low_sum[2 * pairs] = jnp.zeros((GROUP, HALF), jnp.float32)

    @pl.when(me < pairs)
    def _():
        filter_in[me] = filter_send[me]
        waiter(filter_in.at[pl.ds(0, pairs - 1)], filter_sems.at[0], filter_sems.at[1]).wait_recv()

    @pl.when(me >= pairs)
    def _():
        waiter(filter_in, filter_sems.at[0], filter_sems.at[1]).wait_recv()

    def work(piece, _):
        waiter(
            recv.at[pl.ds(0, n - 1), chosen(piece)], out_sems.at[piece], in_sems.at[piece]
        ).wait_recv()

        def one(i, _):
            conv_one(
                piece * PART + i, masks, recv, filter_in, back_out, lag_out,
                base, shift_high, shift_low, weights, accum, low_sum, high_sum,
            )
            return 0

        lax.fori_loop(0, PART, one, 0)
        each_partner(
            lambda other: copy(
                back_out.at[other, chosen(piece)], back_in.at[me, chosen(piece)],
                back_out_sems.at[piece], back_in_sems.at[piece], other,
            ).start()
        )
        back_in[me, chosen(piece)] = back_out[me, chosen(piece)]
        return 0

    lax.fori_loop(0, pieces, work, 0)

    def send_lags(other, _):
        @pl.when(other != me)
        def _():
            copy(
                lag_out.at[other], lag_in.at[me], lag_sems.at[0], lag_sems.at[1], other
            ).start()

        return 0

    lax.fori_loop(0, pairs, send_lags, 0)

    @pl.when(me < pairs)
    def _():
        lag_in[me] = lag_out[me]
        waiter(filter_send.at[pl.ds(0, n - 1)], filter_sems.at[0], filter_sems.at[1]).wait_send()
        waiter(lag_out.at[pl.ds(0, pairs - 1)], lag_sems.at[0], lag_sems.at[1]).wait_send()
        waiter(lag_in.at[pl.ds(0, n - 1)], lag_sems.at[0], lag_sems.at[1]).wait_recv()

    @pl.when(me >= pairs)
    def _():
        lag_in[...] = jnp.zeros_like(lag_in)
        waiter(lag_out, lag_sems.at[0], lag_sems.at[1]).wait_send()

    def finish(piece, _):
        waiter(
            recv.at[pl.ds(0, n - 1), chosen(piece)], out_sems.at[piece], in_sems.at[piece]
        ).wait_send()
        waiter(
            back_in.at[pl.ds(0, n - 1), chosen(piece)], back_out_sems.at[piece],
            back_in_sems.at[piece],
        ).wait()
        return 0

    lax.fori_loop(0, pieces, finish, 0)


def convolve(genomes, query, key, value, grad, filters):
    n, own = filters.shape[:2]
    pairs = n // 2
    pieces = own // PART
    rows = GROUP * n
    padded = rows + 4 * n
    repeats = query.shape[1] // (n * own)
    signals = (n, own, 2, GROUP, HALF)
    vmem = pl.BlockSpec(memory_space=pltpu.VMEM)
    flops = own * 2 * pairs * 2 * rows * 256 * (256 + 128 + 192)
    return pl.pallas_call(
        functools.partial(fused_kernel, repeats),
        in_specs=[pl.BlockSpec(memory_space=pltpu.SMEM)] + [vmem] * 5,
        out_specs=[vmem] * 2,
        out_shape=[
            jax.ShapeDtypeStruct((n, own, GROUP, HALF), jnp.float32),
            jax.ShapeDtypeStruct((n, 2, own, 1, HALF), jnp.float32),
        ],
        scratch_shapes=[
            pltpu.VMEM((n * own * 2 * GROUP, HALF), jnp.float32),
            pltpu.VMEM(signals, jnp.float32),
            pltpu.VMEM((pairs, own, 2, 1, HALF), jnp.float32),
            pltpu.VMEM((n, own, GROUP, HALF), jnp.float32),
            pltpu.VMEM((pairs, 2, own, 1, HALF), jnp.float32),
            pltpu.VMEM((n, rows, HALF), jnp.bfloat16),
            pltpu.VMEM((rows + 16, HALF), jnp.float32),
            pltpu.VMEM((4, padded, HALF), jnp.bfloat16),
            pltpu.VMEM((4, padded, HALF), jnp.bfloat16),
            pltpu.VMEM((pairs // UNROLL, 256 * UNROLL, 256), jnp.bfloat16),
            pltpu.VMEM((rows, 256), jnp.float32),
            pltpu.VMEM((2 * pairs + 1, GROUP, HALF), jnp.float32),
            pltpu.VMEM((2 * pairs, GROUP, HALF), jnp.float32),
            pltpu.SemaphoreType.DMA((2,)),
            pltpu.SemaphoreType.DMA((2,)),
            pltpu.SemaphoreType.DMA((pieces,)),
            pltpu.SemaphoreType.DMA((pieces,)),
            pltpu.SemaphoreType.DMA((pieces,)),
            pltpu.SemaphoreType.DMA((pieces,)),
        ],
        compiler_params=pltpu.CompilerParams(
            collective_id=0, has_side_effects=True, vmem_limit_bytes=52 * 1024 * 1024
        ),
        cost_estimate=pl.CostEstimate(
            flops=flops, bytes_accessed=5 * query.size * 2, transcendentals=0
        ),
    )(genomes, query, key, value, grad, filters)


def local(query_branch, key_branch, value_branch, grad_output, conv_output, filters, genome_blocks):
    rows, channels = query_branch.shape
    width = filters.shape[1]
    repeats = channels // width
    blocks = lax.axis_size("ctx")
    own = width // blocks
    grad_value = (grad_output.astype(jnp.float32) * conv_output.astype(jnp.float32)).astype(
        jnp.bfloat16
    )
    filter_parts = filters.reshape(2, HALF, blocks, own)[:, ::-1].transpose(2, 3, 0, 1)
    back, lag = convolve(
        genome_blocks, query_branch, key_branch, value_branch, grad_output,
        filter_parts[:, :, :, None],
    )
    query32 = query_branch.astype(jnp.float32)
    key32 = key_branch.astype(jnp.float32)
    back = back.reshape(blocks, own, 2, 4, HALF)[:, :, :, :repeats]
    back = back.transpose(2, 4, 3, 0, 1).reshape(rows, channels)
    lag = lag[:, :, :, 0].transpose(1, 3, 0, 2).reshape(rows, width)
    scaled = lag * (rows * blocks) ** (-0.5)
    grad_query = (back * key32).astype(jnp.bfloat16)
    grad_key = (back * query32).astype(jnp.bfloat16)
    grad_filters = lax.psum_scatter(scaled, "ch", scatter_dimension=1, tiled=True)
    return (grad_query, grad_key, grad_value, grad_filters)


def solution(mesh):
    in_specs = (
        P("ctx", "ch"),
        P("ctx", "ch"),
        P("ctx", "ch"),
        P("ctx", "ch"),
        P("ctx", "ch"),
        P("ctx", None),
        P(),
    )
    out_specs = (P("ctx", "ch"), P("ctx", "ch"), P("ctx", "ch"), P("ctx", "ch"))
    return jax.shard_map(local, mesh=mesh, in_specs=in_specs, out_specs=out_specs, check_vma=False)
```

```python
import functools

import jax
import jax.numpy as jnp
from jax import lax
from jax.experimental import pallas as pl
from jax.experimental.pallas import tpu as pltpu
from jax.sharding import PartitionSpec as P

HALF = 128
GROUP = 8
PART = 2
UNROLL = 4
NT = (((1,), (1,)), ((), ()))


def split_bf16(x):
    high = x.astype(jnp.bfloat16)
    low = (x - high.astype(jnp.float32)).astype(jnp.bfloat16)
    return high, low


def make_masks(genomes, masks):
    lags, rows = masks.shape[:2]
    row = lax.broadcasted_iota(jnp.int32, (rows, HALF), 0)

    def owner(place):
        block = lax.shift_right_logical(place, 3)
        found = jnp.zeros((rows, HALF), jnp.int32)
        end = 0
        for g in range(genomes.shape[0]):
            end = end + genomes[g]
            found = found + jnp.where(block >= end, 1, 0)
        return found

    own = owner(row)

    def one(lag, _):
        same = owner(row + 4 * lag) == own
        masks[lag] = jnp.where(same, 1.0, 0.0).astype(jnp.bfloat16)
        return 0

    lax.fori_loop(0, lags, one, 0)


def conv_one(
    f, masks, recv, filter_in, back_out, lag_out,
    base, shift_high, shift_low, weights, accum, low_sum, high_sum,
):
    n = recv.shape[0]
    rows = GROUP * n
    pairs = filter_in.shape[0]
    lane = lax.broadcasted_iota(jnp.int32, (GROUP, HALF), 1)
    place = lax.broadcasted_iota(jnp.int32, (GROUP, HALF), 0)

    base[:rows] = recv[:, f, 0].reshape(rows, HALF)
    for move in range(4):
        high, low = split_bf16(base[4 * move:4 * move + rows])
        shift_high[move, :rows] = high
        shift_low[move, :rows] = low

    def build(c, before):
        for pair in range(UNROLL):
            for side in range(2):
                row = filter_in[c * UNROLL + pair, f, side]
                first = pltpu.roll(
                    jnp.broadcast_to(row, (GROUP, HALF)), 1, 1, stride=1, stride_axis=0
                )
                turned = [first] + [
                    pltpu.roll(first, GROUP * p, 1) for p in range(1, HALF // GROUP)
                ]
                tile = jnp.concatenate(
                    [
                        jnp.where(lane <= place + GROUP * p, turned[p], before[p])
                        for p in range(HALF // GROUP)
                    ],
                    axis=0,
                )
                high, low = split_bf16(tile)
                at = pair * 2 * HALF + side * HALF
                weights[c, at:at + HALF, :HALF] = high
                weights[c, at:at + HALF, HALF:] = low
                before = turned
        return before

    lax.fori_loop(
        0, pairs // UNROLL, build, [jnp.zeros((GROUP, HALF), jnp.float32)] * (HALF // GROUP)
    )

    swap = (
        lax.broadcasted_iota(jnp.int32, (HALF, HALF), 1)
        + lax.broadcasted_iota(jnp.int32, (HALF, HALF), 0)
        == HALF - 1
    ).astype(jnp.bfloat16)
    gated_high, gated_low = split_bf16(recv[:, f, 1].reshape(rows, HALF))
    turned_high = lax.dot_general(
        swap, gated_high, NT, preferred_element_type=jnp.float32
    ).astype(jnp.bfloat16)
    turned_low = lax.dot_general(
        swap, gated_low, NT, preferred_element_type=jnp.float32
    ).astype(jnp.bfloat16)
    turned_both = jnp.concatenate([turned_high, turned_low], axis=0)

    accum[...] = jnp.zeros_like(accum)

    def lag_group(c, _):
        highs, lows = [], []
        for e in range(2 * UNROLL):
            lag = 2 * UNROLL * c + e
            window = pl.ds(pl.multiple_of((2 * UNROLL * c + e - e % 4) * 4, 16), rows)
            mask = masks[lag]
            highs.append(shift_high[e % 4, window] * mask)
            lows.append(shift_low[e % 4, window] * mask)
        high = jnp.concatenate(highs, axis=1)
        low = jnp.concatenate(lows, axis=1)
        accum[...] += jnp.dot(high, weights[c], preferred_element_type=jnp.float32)
        accum[:, :HALF] += jnp.dot(
            low, weights[c, :, :HALF], preferred_element_type=jnp.float32
        )
        both = jnp.dot(turned_both, high, preferred_element_type=jnp.float32)
        outer = (
            both[:HALF] + both[HALF:] + jnp.dot(turned_high, low, preferred_element_type=jnp.float32)
        )
        for side in range(2 * UNROLL):
            here = jnp.zeros((GROUP, HALF), jnp.float32)
            prior = jnp.zeros((GROUP, HALF), jnp.float32)
            for p in range(HALF // GROUP):
                part = outer[GROUP * p:GROUP * p + GROUP, side * HALF:(side + 1) * HALF]
                part = pltpu.roll(part, GROUP * p + 1, 1)
                inside = lane <= GROUP * p
                here = here + jnp.where(inside, part, 0.0)
                prior = prior + jnp.where(inside, 0.0, part)
            here = pltpu.roll(here, 0, 1, stride=1, stride_axis=0)
            prior = pltpu.roll(prior, 0, 1, stride=1, stride_axis=0)
            wrapped = lane < place
            high_sum[2 * UNROLL * c + side] = here + jnp.where(wrapped, prior, 0.0)
            low_sum[2 * UNROLL * c + side] = jnp.where(wrapped, 0.0, prior)
        return 0

    lax.fori_loop(0, pairs // UNROLL, lag_group, 0)
    total = accum[:, :HALF] + accum[:, HALF:]
    back_out[:, f] = total.reshape(n, GROUP, HALF)
    lags = jnp.sum(high_sum[...] + low_sum[1:], axis=1, keepdims=True)
    lag_out[:, :, f] = lags.reshape(pairs, 2, 1, HALF)


def spread_product(first, second, sig, send_rows, repeats):
    channels = first.shape[1]
    width = channels // repeats
    for half in range(2):
        for start in range(0, channels, HALF):
            at = (slice(half * HALF, (half + 1) * HALF), slice(start, start + HALF))
            product = first[at].astype(jnp.float32) * second[at].astype(jnp.float32)
            turn, column = start // width, start % width
            row = column * 2 * GROUP + sig * GROUP + half * 4 + turn
            send_rows[pl.ds(row, HALF, stride=2 * GROUP)] = product.T


def fused_kernel(
    repeats, genomes, query, key, value, grad, filter_send,
    grad_query, grad_key, lag_in,
    send, recv, back_in, filter_in, back_out, lag_out,
    masks, base, shift_high, shift_low, weights, accum, low_sum, high_sum,
    filter_sems, lag_sems, out_sems, in_sems, back_out_sems, back_in_sems,
):
    n, own = filter_send.shape[:2]
    pairs = filter_in.shape[0]
    pieces = own // PART
    me = lax.axis_index("ctx")

    def partner(i):
        return lax.rem(me + i, n)

    def copy(source, target, send_sem, recv_sem, device):
        return pltpu.make_async_remote_copy(
            src_ref=source, dst_ref=target, send_sem=send_sem, recv_sem=recv_sem,
            device_id={"ctx": device}, device_id_type=pl.DeviceIdType.MESH,
        )

    def each_partner(act):
        def step(i, _):
            act(partner(i))
            return 0

        lax.fori_loop(1, n, step, 0)

    def chosen(piece):
        return pl.ds(piece * PART, PART)

    def sent(other, piece):
        count = PART * 2 * GROUP
        start = pl.multiple_of(other * (own * 2 * GROUP) + piece * count, count)
        return send.at[pl.ds(start, count)].reshape(PART, 2, GROUP, HALF)

    def returned(piece):
        count = PART * GROUP
        start = pl.multiple_of(me * (own * GROUP) + piece * count, count)
        return back_in.at[pl.ds(start, count)].reshape(PART, GROUP, HALF)

    def waiter(ref, send_sem, recv_sem):
        return copy(ref, ref, send_sem, recv_sem, partner(1))

    barrier = pltpu.get_barrier_semaphore()
    each_partner(
        lambda other: pl.semaphore_signal(
            barrier, inc=1, device_id={"ctx": other}, device_id_type=pl.DeviceIdType.MESH
        )
    )
    pl.semaphore_wait(barrier, n - 1)

    @pl.when(me < pairs)
    def _():
        each_partner(
            lambda other: copy(
                filter_send.at[other], filter_in.at[me], filter_sems.at[0], filter_sems.at[1], other
            ).start()
        )

    if repeats < 4:
        send[...] = jnp.zeros_like(send)
    spread_product(grad, value, 0, send, repeats)
    spread_product(query, key, 1, send, repeats)

    def send_piece(piece, _):
        each_partner(
            lambda other: copy(
                sent(other, piece), recv.at[me, chosen(piece)],
                out_sems.at[piece], in_sems.at[piece], other,
            ).start()
        )
        return 0

    lax.fori_loop(0, pieces, send_piece, 0)

    mine = send[pl.ds(pl.multiple_of(me * (own * 2 * GROUP), 16), own * 2 * GROUP)]
    recv[me] = mine.reshape(own, 2, GROUP, HALF)
    make_masks(genomes, masks)
    base[...] = jnp.zeros_like(base)
    shift_high[...] = jnp.zeros_like(shift_high)
    shift_low[...] = jnp.zeros_like(shift_low)
    low_sum[2 * pairs] = jnp.zeros((GROUP, HALF), jnp.float32)

    @pl.when(me < pairs)
    def _():
        filter_in[me] = filter_send[me]
        waiter(filter_in.at[pl.ds(0, pairs - 1)], filter_sems.at[0], filter_sems.at[1]).wait_recv()

    @pl.when(me >= pairs)
    def _():
        waiter(filter_in, filter_sems.at[0], filter_sems.at[1]).wait_recv()

    def work(piece, _):
        waiter(
            recv.at[pl.ds(0, n - 1), chosen(piece)], out_sems.at[piece], in_sems.at[piece]
        ).wait_recv()

        def one(i, _):
            conv_one(
                piece * PART + i, masks, recv, filter_in, back_out, lag_out,
                base, shift_high, shift_low, weights, accum, low_sum, high_sum,
            )
            return 0

        lax.fori_loop(0, PART, one, 0)
        each_partner(
            lambda other: copy(
                back_out.at[other, chosen(piece)], returned(piece),
                back_out_sems.at[piece], back_in_sems.at[piece], other,
            ).start()
        )
        start = pl.multiple_of(me * (own * GROUP) + piece * (PART * GROUP), PART * GROUP)
        back_in[pl.ds(start, PART * GROUP)] = back_out[me, chosen(piece)].reshape(
            PART * GROUP, HALF
        )

        def send_lags(other, _):
            @pl.when(other != me)
            def _():
                copy(
                    lag_out.at[other, :, chosen(piece)], lag_in.at[me, :, chosen(piece)],
                    lag_sems.at[0], lag_sems.at[1], other,
                ).start()

            return 0

        lax.fori_loop(0, pairs, send_lags, 0)
        return 0

    lax.fori_loop(0, pieces, work, 0)

    @pl.when(me < pairs)
    def _():
        lag_in[me] = lag_out[me]
        waiter(filter_send.at[pl.ds(0, n - 1)], filter_sems.at[0], filter_sems.at[1]).wait_send()
        waiter(lag_out.at[pl.ds(0, pairs - 1)], lag_sems.at[0], lag_sems.at[1]).wait_send()
        waiter(lag_in.at[pl.ds(0, n - 1)], lag_sems.at[0], lag_sems.at[1]).wait_recv()

    @pl.when(me >= pairs)
    def _():
        lag_in[...] = jnp.zeros_like(lag_in)
        waiter(lag_out, lag_sems.at[0], lag_sems.at[1]).wait_send()

    def finish(piece, _):
        waiter(
            recv.at[pl.ds(0, n - 1), chosen(piece)], out_sems.at[piece], in_sems.at[piece]
        ).wait_send()
        waiter(
            back_out.at[pl.ds(0, n - 1), chosen(piece)], back_out_sems.at[piece],
            back_in_sems.at[piece],
        ).wait()
        return 0

    lax.fori_loop(0, pieces, finish, 0)
    channels = query.shape[1]
    width = channels // repeats
    for half in range(2):
        for start in range(0, channels, HALF):
            at = (slice(half * HALF, (half + 1) * HALF), slice(start, start + HALF))
            row = start % width * GROUP + half * 4 + start // width
            back = back_in[pl.ds(row, HALF, stride=GROUP)].T
            grad_query[at] = (back * key[at].astype(jnp.float32)).astype(jnp.bfloat16)
            grad_key[at] = (back * query[at].astype(jnp.float32)).astype(jnp.bfloat16)


def convolve(genomes, query, key, value, grad, filters):
    n, own = filters.shape[:2]
    pairs = n // 2
    pieces = own // PART
    rows = GROUP * n
    padded = rows + 4 * n
    repeats = query.shape[1] // (n * own)
    signals = (n, own, 2, GROUP, HALF)
    vmem = pl.BlockSpec(memory_space=pltpu.VMEM)
    flops = own * 2 * pairs * 2 * rows * 256 * (256 + 128 + 192)
    return pl.pallas_call(
        functools.partial(fused_kernel, repeats),
        in_specs=[pl.BlockSpec(memory_space=pltpu.SMEM)] + [vmem] * 5,
        out_specs=[vmem] * 3,
        out_shape=[
            jax.ShapeDtypeStruct(query.shape, jnp.bfloat16),
            jax.ShapeDtypeStruct(query.shape, jnp.bfloat16),
            jax.ShapeDtypeStruct((n, 2, own, 1, HALF), jnp.float32),
        ],
        scratch_shapes=[
            pltpu.VMEM((n * own * 2 * GROUP, HALF), jnp.float32),
            pltpu.VMEM(signals, jnp.float32),
            pltpu.VMEM((n * own * GROUP, HALF), jnp.float32),
            pltpu.VMEM((pairs, own, 2, 1, HALF), jnp.float32),
            pltpu.VMEM((n, own, GROUP, HALF), jnp.float32),
            pltpu.VMEM((pairs, 2, own, 1, HALF), jnp.float32),
            pltpu.VMEM((n, rows, HALF), jnp.bfloat16),
            pltpu.VMEM((rows + 16, HALF), jnp.float32),
            pltpu.VMEM((4, padded, HALF), jnp.bfloat16),
            pltpu.VMEM((4, padded, HALF), jnp.bfloat16),
            pltpu.VMEM((pairs // UNROLL, 256 * UNROLL, 256), jnp.bfloat16),
            pltpu.VMEM((rows, 256), jnp.float32),
            pltpu.VMEM((2 * pairs + 1, GROUP, HALF), jnp.float32),
            pltpu.VMEM((2 * pairs, GROUP, HALF), jnp.float32),
            pltpu.SemaphoreType.DMA((2,)),
            pltpu.SemaphoreType.DMA((2,)),
            pltpu.SemaphoreType.DMA((pieces,)),
            pltpu.SemaphoreType.DMA((pieces,)),
            pltpu.SemaphoreType.DMA((pieces,)),
            pltpu.SemaphoreType.DMA((pieces,)),
        ],
        compiler_params=pltpu.CompilerParams(
            collective_id=0, has_side_effects=True, vmem_limit_bytes=52 * 1024 * 1024
        ),
        cost_estimate=pl.CostEstimate(
            flops=flops, bytes_accessed=5 * query.size * 2, transcendentals=0
        ),
    )(genomes, query, key, value, grad, filters)


def local(query_branch, key_branch, value_branch, grad_output, conv_output, filters, genome_blocks):
    rows, channels = query_branch.shape
    width = filters.shape[1]
    blocks = lax.axis_size("ctx")
    own = width // blocks
    grad_value = (grad_output.astype(jnp.float32) * conv_output.astype(jnp.float32)).astype(
        jnp.bfloat16
    )
    filter_parts = filters.reshape(2, HALF, blocks, own)[:, ::-1].transpose(2, 3, 0, 1)
    grad_query, grad_key, lag = convolve(
        genome_blocks, query_branch, key_branch, value_branch, grad_output,
        filter_parts[:, :, :, None],
    )
    lag = lag[:, :, :, 0].transpose(1, 3, 0, 2).reshape(rows, width)
    scaled = lag * (rows * blocks) ** (-0.5)
    grad_filters = lax.psum_scatter(scaled, "ch", scatter_dimension=1, tiled=True)
    return (grad_query, grad_key, grad_value, grad_filters)


def solution(mesh):
    in_specs = (
        P("ctx", "ch"),
        P("ctx", "ch"),
        P("ctx", "ch"),
        P("ctx", "ch"),
        P("ctx", "ch"),
        P("ctx", None),
        P(),
    )
    out_specs = (P("ctx", "ch"), P("ctx", "ch"), P("ctx", "ch"), P("ctx", "ch"))
    return jax.shard_map(local, mesh=mesh, in_specs=in_specs, out_specs=out_specs, check_vma=False)
```

```python
import functools

import jax
import jax.numpy as jnp
from jax import lax
from jax.experimental import pallas as pl
from jax.experimental.pallas import tpu as pltpu
from jax.sharding import PartitionSpec as P

HALF = 128
GROUP = 8
PART = 2
UNROLL = 4
STRIDE = 13
EARLY = 2
NT = (((1,), (1,)), ((), ()))


def split_bf16(x):
    high = x.astype(jnp.bfloat16)
    low = (x - high.astype(jnp.float32)).astype(jnp.bfloat16)
    return high, low


def make_masks(genomes, masks):
    lags, rows = masks.shape[:2]
    row = lax.broadcasted_iota(jnp.int32, (rows, HALF), 0)

    def owner(place):
        block = lax.shift_right_logical(place, 3)
        found = jnp.zeros((rows, HALF), jnp.int32)
        end = 0
        for g in range(genomes.shape[0]):
            end = end + genomes[g]
            found = found + jnp.where(block >= end, 1, 0)
        return found

    own = owner(row)

    def one(lag, _):
        same = owner(row + 4 * lag) == own
        masks[lag] = jnp.where(same, 1.0, 0.0).astype(jnp.bfloat16)
        return 0

    lax.fori_loop(0, lags, one, 0)


def conv_one(
    f, masks, recv, filter_in, back_out, lag_out,
    base, shift_high, shift_low, weights, accum, low_sum, high_sum,
):
    n = recv.shape[0]
    rows = GROUP * n
    pairs = filter_in.shape[0]
    lane = lax.broadcasted_iota(jnp.int32, (GROUP, HALF), 1)
    place = lax.broadcasted_iota(jnp.int32, (GROUP, HALF), 0)

    base[:rows] = recv[:, f, 0].reshape(rows, HALF)
    for move in range(4):
        high, low = split_bf16(base[4 * move:4 * move + rows])
        shift_high[move, :rows] = high
        shift_low[move, :rows] = low

    def build(c, before):
        for pair in range(UNROLL):
            for side in range(2):
                row = filter_in[c * UNROLL + pair, f, side]
                first = pltpu.roll(
                    jnp.broadcast_to(row, (GROUP, HALF)), 1, 1, stride=1, stride_axis=0
                )
                turned = [first] + [
                    pltpu.roll(first, GROUP * p, 1) for p in range(1, HALF // GROUP)
                ]
                tile = jnp.concatenate(
                    [
                        jnp.where(lane <= place + GROUP * p, turned[p], before[p])
                        for p in range(HALF // GROUP)
                    ],
                    axis=0,
                )
                high, low = split_bf16(tile)
                at = pair * 2 * HALF + side * HALF
                weights[c, at:at + HALF, :HALF] = high
                weights[c, at:at + HALF, HALF:] = low
                before = turned
        return before

    lax.fori_loop(
        0, pairs // UNROLL, build, [jnp.zeros((GROUP, HALF), jnp.float32)] * (HALF // GROUP)
    )

    swap = (
        lax.broadcasted_iota(jnp.int32, (HALF, HALF), 1)
        + lax.broadcasted_iota(jnp.int32, (HALF, HALF), 0)
        == HALF - 1
    ).astype(jnp.bfloat16)
    gated_high, gated_low = split_bf16(recv[:, f, 1].reshape(rows, HALF))
    turned_high = lax.dot_general(
        swap, gated_high, NT, preferred_element_type=jnp.float32
    ).astype(jnp.bfloat16)
    turned_low = lax.dot_general(
        swap, gated_low, NT, preferred_element_type=jnp.float32
    ).astype(jnp.bfloat16)
    turned_both = jnp.concatenate([turned_high, turned_low], axis=0)

    accum[...] = jnp.zeros_like(accum)

    def lag_group(c, _):
        highs, lows = [], []
        for e in range(2 * UNROLL):
            lag = 2 * UNROLL * c + e
            window = pl.ds(pl.multiple_of((2 * UNROLL * c + e - e % 4) * 4, 16), rows)
            mask = masks[lag]
            highs.append(shift_high[e % 4, window] * mask)
            lows.append(shift_low[e % 4, window] * mask)
        high = jnp.concatenate(highs, axis=1)
        low = jnp.concatenate(lows, axis=1)
        accum[...] += jnp.dot(high, weights[c], preferred_element_type=jnp.float32)
        accum[:, :HALF] += jnp.dot(
            low, weights[c, :, :HALF], preferred_element_type=jnp.float32
        )
        both = jnp.dot(turned_both, high, preferred_element_type=jnp.float32)
        outer = (
            both[:HALF] + both[HALF:] + jnp.dot(turned_high, low, preferred_element_type=jnp.float32)
        )
        for side in range(2 * UNROLL):
            here = jnp.zeros((GROUP, HALF), jnp.float32)
            prior = jnp.zeros((GROUP, HALF), jnp.float32)
            for p in range(HALF // GROUP):
                part = outer[GROUP * p:GROUP * p + GROUP, side * HALF:(side + 1) * HALF]
                part = pltpu.roll(part, GROUP * p + 1, 1)
                inside = lane <= GROUP * p
                here = here + jnp.where(inside, part, 0.0)
                prior = prior + jnp.where(inside, 0.0, part)
            here = pltpu.roll(here, 0, 1, stride=1, stride_axis=0)
            prior = pltpu.roll(prior, 0, 1, stride=1, stride_axis=0)
            wrapped = lane < place
            high_sum[2 * UNROLL * c + side] = here + jnp.where(wrapped, prior, 0.0)
            low_sum[2 * UNROLL * c + side] = jnp.where(wrapped, 0.0, prior)
        return 0

    lax.fori_loop(0, pairs // UNROLL, lag_group, 0)
    total = accum[:, :HALF] + accum[:, HALF:]
    back_out[:, f] = total.reshape(n, GROUP, HALF)
    lags = jnp.sum(high_sum[...] + low_sum[1:], axis=1, keepdims=True)
    lag_out[:, :, f] = lags.reshape(pairs, 2, 1, HALF)


def spread_product(first, second, sig, send_rows, repeats):
    channels = first.shape[1]
    width = channels // repeats
    for half in range(2):
        for start in range(0, channels, HALF):
            at = (slice(half * HALF, (half + 1) * HALF), slice(start, start + HALF))
            product = first[at].astype(jnp.float32) * second[at].astype(jnp.float32)
            turn, column = start // width, start % width
            row = column * 2 * GROUP + sig * GROUP + half * 4 + turn
            send_rows[pl.ds(row, HALF, stride=2 * GROUP)] = product.T


def fused_kernel(
    repeats, genomes, query, key, value, grad, filter_send,
    grad_query, grad_key, lag_in,
    send, recv, back_in, filter_in, back_out, lag_out,
    masks, base, shift_high, shift_low, weights, accum, low_sum, high_sum,
    filter_sems, lag_sems, out_sems, in_sems, back_out_sems, back_in_sems,
):
    n, own = filter_send.shape[:2]
    pairs = filter_in.shape[0]
    pieces = own // PART
    me = lax.axis_index("ctx")

    def partner(i):
        return lax.rem(me + STRIDE * i, n)

    def copy(source, target, send_sem, recv_sem, device):
        return pltpu.make_async_remote_copy(
            src_ref=source, dst_ref=target, send_sem=send_sem, recv_sem=recv_sem,
            device_id={"ctx": device}, device_id_type=pl.DeviceIdType.MESH,
        )

    def each_partner(act):
        def step(i, _):
            act(partner(i))
            return 0

        lax.fori_loop(1, n, step, 0)

    def chosen(piece):
        return pl.ds(piece * PART, PART)

    def sent(other, piece):
        count = PART * 2 * GROUP
        start = pl.multiple_of(other * (own * 2 * GROUP) + piece * count, count)
        return send.at[pl.ds(start, count)].reshape(PART, 2, GROUP, HALF)

    def returned(piece):
        count = PART * GROUP
        start = pl.multiple_of(me * (own * GROUP) + piece * count, count)
        return back_in.at[pl.ds(start, count)].reshape(PART, GROUP, HALF)

    def waiter(ref, send_sem, recv_sem):
        return copy(ref, ref, send_sem, recv_sem, partner(1))

    barrier = pltpu.get_barrier_semaphore()
    each_partner(
        lambda other: pl.semaphore_signal(
            barrier, inc=1, device_id={"ctx": other}, device_id_type=pl.DeviceIdType.MESH
        )
    )
    pl.semaphore_wait(barrier, n - 1)

    @pl.when(me < pairs)
    def _():
        each_partner(
            lambda other: copy(
                filter_send.at[other], filter_in.at[me], filter_sems.at[0], filter_sems.at[1], other
            ).start()
        )

    if repeats < 4:
        send[...] = jnp.zeros_like(send)

    def send_half(sig):
        def one(piece, _):
            each_partner(
                lambda other: copy(
                    sent(other, piece).at[:, sig], recv.at[me, chosen(piece), sig],
                    out_sems.at[piece], in_sems.at[piece], other,
                ).start()
            )
            return 0

        lax.fori_loop(0, EARLY, one, 0)

    def send_piece(piece, _):
        each_partner(
            lambda other: copy(
                sent(other, piece), recv.at[me, chosen(piece)],
                out_sems.at[piece], in_sems.at[piece], other,
            ).start()
        )
        return 0

    spread_product(grad, value, 0, send, repeats)
    send_half(0)
    spread_product(query, key, 1, send, repeats)
    send_half(1)
    lax.fori_loop(EARLY, pieces, send_piece, 0)

    mine = send[pl.ds(pl.multiple_of(me * (own * 2 * GROUP), 16), own * 2 * GROUP)]
    recv[me] = mine.reshape(own, 2, GROUP, HALF)
    make_masks(genomes, masks)
    base[...] = jnp.zeros_like(base)
    shift_high[...] = jnp.zeros_like(shift_high)
    shift_low[...] = jnp.zeros_like(shift_low)
    low_sum[2 * pairs] = jnp.zeros((GROUP, HALF), jnp.float32)

    @pl.when(me < pairs)
    def _():
        filter_in[me] = filter_send[me]
        waiter(filter_in.at[pl.ds(0, pairs - 1)], filter_sems.at[0], filter_sems.at[1]).wait_recv()

    @pl.when(me >= pairs)
    def _():
        waiter(filter_in, filter_sems.at[0], filter_sems.at[1]).wait_recv()

    def work(piece, _):
        waiter(
            recv.at[pl.ds(0, n - 1), chosen(piece)], out_sems.at[piece], in_sems.at[piece]
        ).wait_recv()

        def one(i, _):
            conv_one(
                piece * PART + i, masks, recv, filter_in, back_out, lag_out,
                base, shift_high, shift_low, weights, accum, low_sum, high_sum,
            )
            return 0

        lax.fori_loop(0, PART, one, 0)
        each_partner(
            lambda other: copy(
                back_out.at[other, chosen(piece)], returned(piece),
                back_out_sems.at[piece], back_in_sems.at[piece], other,
            ).start()
        )
        start = pl.multiple_of(me * (own * GROUP) + piece * (PART * GROUP), PART * GROUP)
        back_in[pl.ds(start, PART * GROUP)] = back_out[me, chosen(piece)].reshape(
            PART * GROUP, HALF
        )

        def send_lags(other, _):
            @pl.when(other != me)
            def _():
                copy(
                    lag_out.at[other, :, chosen(piece)], lag_in.at[me, :, chosen(piece)],
                    lag_sems.at[0], lag_sems.at[1], other,
                ).start()

            return 0

        lax.fori_loop(0, pairs, send_lags, 0)
        return 0

    lax.fori_loop(0, pieces, work, 0)

    @pl.when(me < pairs)
    def _():
        lag_in[me] = lag_out[me]
        waiter(filter_send.at[pl.ds(0, n - 1)], filter_sems.at[0], filter_sems.at[1]).wait_send()
        waiter(lag_out.at[pl.ds(0, pairs - 1)], lag_sems.at[0], lag_sems.at[1]).wait_send()
        waiter(lag_in.at[pl.ds(0, n - 1)], lag_sems.at[0], lag_sems.at[1]).wait_recv()

    @pl.when(me >= pairs)
    def _():
        lag_in[...] = jnp.zeros_like(lag_in)
        waiter(lag_out, lag_sems.at[0], lag_sems.at[1]).wait_send()

    def finish(piece, _):
        waiter(
            recv.at[pl.ds(0, n - 1), chosen(piece)], out_sems.at[piece], in_sems.at[piece]
        ).wait_send()
        waiter(
            back_out.at[pl.ds(0, n - 1), chosen(piece)], back_out_sems.at[piece],
            back_in_sems.at[piece],
        ).wait()
        return 0

    lax.fori_loop(0, pieces, finish, 0)
    channels = query.shape[1]
    width = channels // repeats
    for half in range(2):
        for start in range(0, channels, HALF):
            at = (slice(half * HALF, (half + 1) * HALF), slice(start, start + HALF))
            row = start % width * GROUP + half * 4 + start // width
            back = back_in[pl.ds(row, HALF, stride=GROUP)].T
            grad_query[at] = (back * key[at].astype(jnp.float32)).astype(jnp.bfloat16)
            grad_key[at] = (back * query[at].astype(jnp.float32)).astype(jnp.bfloat16)


def convolve(genomes, query, key, value, grad, filters):
    n, own = filters.shape[:2]
    pairs = n // 2
    pieces = own // PART
    rows = GROUP * n
    padded = rows + 4 * n
    repeats = query.shape[1] // (n * own)
    signals = (n, own, 2, GROUP, HALF)
    vmem = pl.BlockSpec(memory_space=pltpu.VMEM)
    flops = own * 2 * pairs * 2 * rows * 256 * (256 + 128 + 192)
    return pl.pallas_call(
        functools.partial(fused_kernel, repeats),
        in_specs=[pl.BlockSpec(memory_space=pltpu.SMEM)] + [vmem] * 5,
        out_specs=[vmem] * 3,
        out_shape=[
            jax.ShapeDtypeStruct(query.shape, jnp.bfloat16),
            jax.ShapeDtypeStruct(query.shape, jnp.bfloat16),
            jax.ShapeDtypeStruct((n, 2, own, 1, HALF), jnp.float32),
        ],
        scratch_shapes=[
            pltpu.VMEM((n * own * 2 * GROUP, HALF), jnp.float32),
            pltpu.VMEM(signals, jnp.float32),
            pltpu.VMEM((n * own * GROUP, HALF), jnp.float32),
            pltpu.VMEM((pairs, own, 2, 1, HALF), jnp.float32),
            pltpu.VMEM((n, own, GROUP, HALF), jnp.float32),
            pltpu.VMEM((pairs, 2, own, 1, HALF), jnp.float32),
            pltpu.VMEM((n, rows, HALF), jnp.bfloat16),
            pltpu.VMEM((rows + 16, HALF), jnp.float32),
            pltpu.VMEM((4, padded, HALF), jnp.bfloat16),
            pltpu.VMEM((4, padded, HALF), jnp.bfloat16),
            pltpu.VMEM((pairs // UNROLL, 256 * UNROLL, 256), jnp.bfloat16),
            pltpu.VMEM((rows, 256), jnp.float32),
            pltpu.VMEM((2 * pairs + 1, GROUP, HALF), jnp.float32),
            pltpu.VMEM((2 * pairs, GROUP, HALF), jnp.float32),
            pltpu.SemaphoreType.DMA((2,)),
            pltpu.SemaphoreType.DMA((2,)),
            pltpu.SemaphoreType.DMA((pieces,)),
            pltpu.SemaphoreType.DMA((pieces,)),
            pltpu.SemaphoreType.DMA((pieces,)),
            pltpu.SemaphoreType.DMA((pieces,)),
        ],
        compiler_params=pltpu.CompilerParams(
            collective_id=0, has_side_effects=True, vmem_limit_bytes=52 * 1024 * 1024
        ),
        cost_estimate=pl.CostEstimate(
            flops=flops, bytes_accessed=5 * query.size * 2, transcendentals=0
        ),
    )(genomes, query, key, value, grad, filters)


def local(query_branch, key_branch, value_branch, grad_output, conv_output, filters, genome_blocks):
    rows, channels = query_branch.shape
    width = filters.shape[1]
    blocks = lax.axis_size("ctx")
    own = width // blocks
    grad_value = (grad_output.astype(jnp.float32) * conv_output.astype(jnp.float32)).astype(
        jnp.bfloat16
    )
    filter_parts = filters.reshape(2, HALF, blocks, own)[:, ::-1].transpose(2, 3, 0, 1)
    grad_query, grad_key, lag = convolve(
        genome_blocks, query_branch, key_branch, value_branch, grad_output,
        filter_parts[:, :, :, None],
    )
    lag = lag[:, :, :, 0].transpose(1, 3, 0, 2).reshape(rows, width)
    scaled = lag * (rows * blocks) ** (-0.5)
    grad_filters = lax.psum_scatter(scaled, "ch", scatter_dimension=1, tiled=True)
    return (grad_query, grad_key, grad_value, grad_filters)


def solution(mesh):
    in_specs = (
        P("ctx", "ch"),
        P("ctx", "ch"),
        P("ctx", "ch"),
        P("ctx", "ch"),
        P("ctx", "ch"),
        P("ctx", None),
        P(),
    )
    out_specs = (P("ctx", "ch"), P("ctx", "ch"), P("ctx", "ch"), P("ctx", "ch"))
    return jax.shard_map(local, mesh=mesh, in_specs=in_specs, out_specs=out_specs, check_vma=False)
```

```python
import functools

import jax
import jax.numpy as jnp
from jax import lax
from jax.experimental import pallas as pl
from jax.experimental.pallas import tpu as pltpu
from jax.sharding import PartitionSpec as P

HALF = 128
GROUP = 8
PART = 2
UNROLL = 4
STRIDE = 13
EARLY = 2
NT = (((1,), (1,)), ((), ()))


def split_bf16(x):
    high = x.astype(jnp.bfloat16)
    low = (x - high.astype(jnp.float32)).astype(jnp.bfloat16)
    return high, low


def make_masks(genomes, masks):
    lags, rows = masks.shape[:2]
    row = lax.broadcasted_iota(jnp.int32, (rows, HALF), 0)

    def owner(place):
        block = lax.shift_right_logical(place, 3)
        found = jnp.zeros((rows, HALF), jnp.int32)
        end = 0
        for g in range(genomes.shape[0]):
            end = end + genomes[g]
            found = found + jnp.where(block >= end, 1, 0)
        return found

    own = owner(row)

    def one(lag, _):
        same = owner(row + 4 * lag) == own
        masks[lag] = jnp.where(same, 1.0, 0.0).astype(jnp.bfloat16)
        return 0

    lax.fori_loop(0, lags, one, 0)


def conv_one(
    f, masks, recv, filter_in, back_out, lag_out,
    base, shift_high, shift_low, weights, accum, low_sum, high_sum,
):
    n = recv.shape[0]
    rows = GROUP * n
    pairs = filter_in.shape[0]
    lane = lax.broadcasted_iota(jnp.int32, (GROUP, HALF), 1)
    place = lax.broadcasted_iota(jnp.int32, (GROUP, HALF), 0)

    base[:rows] = recv[:, f, 0].reshape(rows, HALF)
    for move in range(4):
        high, low = split_bf16(base[4 * move:4 * move + rows])
        shift_high[move, :rows] = high
        shift_low[move, :rows] = low

    def build(c, before):
        for pair in range(UNROLL):
            for side in range(2):
                row = filter_in[c * UNROLL + pair, f, side]
                first = pltpu.roll(
                    jnp.broadcast_to(row, (GROUP, HALF)), 1, 1, stride=1, stride_axis=0
                )
                turned = [first] + [
                    pltpu.roll(first, GROUP * p, 1) for p in range(1, HALF // GROUP)
                ]
                tile = jnp.concatenate(
                    [
                        jnp.where(lane <= place + GROUP * p, turned[p], before[p])
                        for p in range(HALF // GROUP)
                    ],
                    axis=0,
                )
                high, low = split_bf16(tile)
                at = pair * 2 * HALF + side * HALF
                weights[c, at:at + HALF, :HALF] = high
                weights[c, at:at + HALF, HALF:] = low
                before = turned
        return before

    lax.fori_loop(
        0, pairs // UNROLL, build, [jnp.zeros((GROUP, HALF), jnp.float32)] * (HALF // GROUP)
    )

    swap = (
        lax.broadcasted_iota(jnp.int32, (HALF, HALF), 1)
        + lax.broadcasted_iota(jnp.int32, (HALF, HALF), 0)
        == HALF - 1
    ).astype(jnp.bfloat16)
    gated_high, gated_low = split_bf16(recv[:, f, 1].reshape(rows, HALF))
    turned_high = lax.dot_general(
        swap, gated_high, NT, preferred_element_type=jnp.float32
    ).astype(jnp.bfloat16)
    turned_low = lax.dot_general(
        swap, gated_low, NT, preferred_element_type=jnp.float32
    ).astype(jnp.bfloat16)
    turned_both = jnp.concatenate([turned_high, turned_low], axis=0)

    accum[...] = jnp.zeros_like(accum)

    def lag_group(c, _):
        highs, lows = [], []
        for e in range(2 * UNROLL):
            lag = 2 * UNROLL * c + e
            window = pl.ds(pl.multiple_of((2 * UNROLL * c + e - e % 4) * 4, 16), rows)
            mask = masks[lag]
            highs.append(shift_high[e % 4, window] * mask)
            lows.append(shift_low[e % 4, window] * mask)
        high = jnp.concatenate(highs, axis=1)
        low = jnp.concatenate(lows, axis=1)
        accum[...] += jnp.dot(
            jnp.concatenate([high, low], axis=0), weights[c], preferred_element_type=jnp.float32
        )
        both = jnp.dot(turned_both, high, preferred_element_type=jnp.float32)
        outer = (
            both[:HALF] + both[HALF:] + jnp.dot(turned_high, low, preferred_element_type=jnp.float32)
        )
        for side in range(2 * UNROLL):
            here = jnp.zeros((GROUP, HALF), jnp.float32)
            prior = jnp.zeros((GROUP, HALF), jnp.float32)
            for p in range(HALF // GROUP):
                part = outer[GROUP * p:GROUP * p + GROUP, side * HALF:(side + 1) * HALF]
                part = pltpu.roll(part, GROUP * p + 1, 1)
                inside = lane <= GROUP * p
                here = here + jnp.where(inside, part, 0.0)
                prior = prior + jnp.where(inside, 0.0, part)
            here = pltpu.roll(here, 0, 1, stride=1, stride_axis=0)
            prior = pltpu.roll(prior, 0, 1, stride=1, stride_axis=0)
            wrapped = lane < place
            high_sum[2 * UNROLL * c + side] = here + jnp.where(wrapped, prior, 0.0)
            low_sum[2 * UNROLL * c + side] = jnp.where(wrapped, 0.0, prior)
        return 0

    lax.fori_loop(0, pairs // UNROLL, lag_group, 0)
    total = (
        accum[:rows, :HALF] + accum[:rows, HALF:] + accum[rows:, :HALF] + accum[rows:, HALF:]
    )
    back_out[:, f] = total.reshape(n, GROUP, HALF)
    lags = jnp.sum(high_sum[...] + low_sum[1:], axis=1, keepdims=True)
    lag_out[:, :, f] = lags.reshape(pairs, 2, 1, HALF)


def spread_product(first, second, sig, send_rows, repeats):
    channels = first.shape[1]
    width = channels // repeats
    for half in range(2):
        for start in range(0, channels, HALF):
            at = (slice(half * HALF, (half + 1) * HALF), slice(start, start + HALF))
            product = first[at].astype(jnp.float32) * second[at].astype(jnp.float32)
            turn, column = start // width, start % width
            row = column * 2 * GROUP + sig * GROUP + half * 4 + turn
            send_rows[pl.ds(row, HALF, stride=2 * GROUP)] = product.T


def fused_kernel(
    repeats, genomes, query, key, value, grad, filter_send,
    grad_query, grad_key, lag_in,
    send, recv, back_in, filter_in, back_out, lag_out,
    masks, base, shift_high, shift_low, weights, accum, low_sum, high_sum,
    filter_sems, lag_sems, out_sems, in_sems, back_out_sems, back_in_sems,
):
    n, own = filter_send.shape[:2]
    pairs = filter_in.shape[0]
    pieces = own // PART
    me = lax.axis_index("ctx")

    def partner(i):
        return lax.rem(me + STRIDE * i, n)

    def copy(source, target, send_sem, recv_sem, device):
        return pltpu.make_async_remote_copy(
            src_ref=source, dst_ref=target, send_sem=send_sem, recv_sem=recv_sem,
            device_id={"ctx": device}, device_id_type=pl.DeviceIdType.MESH,
        )

    def each_partner(act):
        def step(i, _):
            act(partner(i))
            return 0

        lax.fori_loop(1, n, step, 0)

    def chosen(piece):
        return pl.ds(piece * PART, PART)

    def sent(other, piece):
        count = PART * 2 * GROUP
        start = pl.multiple_of(other * (own * 2 * GROUP) + piece * count, count)
        return send.at[pl.ds(start, count)].reshape(PART, 2, GROUP, HALF)

    def returned(piece):
        count = PART * GROUP
        start = pl.multiple_of(me * (own * GROUP) + piece * count, count)
        return back_in.at[pl.ds(start, count)].reshape(PART, GROUP, HALF)

    def waiter(ref, send_sem, recv_sem):
        return copy(ref, ref, send_sem, recv_sem, partner(1))

    barrier = pltpu.get_barrier_semaphore()
    each_partner(
        lambda other: pl.semaphore_signal(
            barrier, inc=1, device_id={"ctx": other}, device_id_type=pl.DeviceIdType.MESH
        )
    )
    pl.semaphore_wait(barrier, n - 1)

    @pl.when(me < pairs)
    def _():
        each_partner(
            lambda other: copy(
                filter_send.at[other], filter_in.at[me], filter_sems.at[0], filter_sems.at[1], other
            ).start()
        )

    if repeats < 4:
        send[...] = jnp.zeros_like(send)

    def send_half(sig):
        def one(piece, _):
            each_partner(
                lambda other: copy(
                    sent(other, piece).at[:, sig], recv.at[me, chosen(piece), sig],
                    out_sems.at[piece], in_sems.at[piece], other,
                ).start()
            )
            return 0

        lax.fori_loop(0, EARLY, one, 0)

    def send_piece(piece, _):
        each_partner(
            lambda other: copy(
                sent(other, piece), recv.at[me, chosen(piece)],
                out_sems.at[piece], in_sems.at[piece], other,
            ).start()
        )
        return 0

    spread_product(grad, value, 0, send, repeats)
    send_half(0)
    spread_product(query, key, 1, send, repeats)
    send_half(1)
    lax.fori_loop(EARLY, pieces, send_piece, 0)

    mine = send[pl.ds(pl.multiple_of(me * (own * 2 * GROUP), 16), own * 2 * GROUP)]
    recv[me] = mine.reshape(own, 2, GROUP, HALF)
    make_masks(genomes, masks)
    base[...] = jnp.zeros_like(base)
    shift_high[...] = jnp.zeros_like(shift_high)
    shift_low[...] = jnp.zeros_like(shift_low)
    low_sum[2 * pairs] = jnp.zeros((GROUP, HALF), jnp.float32)

    @pl.when(me < pairs)
    def _():
        filter_in[me] = filter_send[me]
        waiter(filter_in.at[pl.ds(0, pairs - 1)], filter_sems.at[0], filter_sems.at[1]).wait_recv()

    @pl.when(me >= pairs)
    def _():
        waiter(filter_in, filter_sems.at[0], filter_sems.at[1]).wait_recv()

    def work(piece, _):
        waiter(
            recv.at[pl.ds(0, n - 1), chosen(piece)], out_sems.at[piece], in_sems.at[piece]
        ).wait_recv()

        def one(i, _):
            conv_one(
                piece * PART + i, masks, recv, filter_in, back_out, lag_out,
                base, shift_high, shift_low, weights, accum, low_sum, high_sum,
            )
            return 0

        lax.fori_loop(0, PART, one, 0)
        each_partner(
            lambda other: copy(
                back_out.at[other, chosen(piece)], returned(piece),
                back_out_sems.at[piece], back_in_sems.at[piece], other,
            ).start()
        )
        start = pl.multiple_of(me * (own * GROUP) + piece * (PART * GROUP), PART * GROUP)
        back_in[pl.ds(start, PART * GROUP)] = back_out[me, chosen(piece)].reshape(
            PART * GROUP, HALF
        )

        def send_lags(other, _):
            @pl.when(other != me)
            def _():
                copy(
                    lag_out.at[other, :, chosen(piece)], lag_in.at[me, :, chosen(piece)],
                    lag_sems.at[0], lag_sems.at[1], other,
                ).start()

            return 0

        lax.fori_loop(0, pairs, send_lags, 0)
        return 0

    lax.fori_loop(0, pieces, work, 0)

    @pl.when(me < pairs)
    def _():
        lag_in[me] = lag_out[me]
        waiter(filter_send.at[pl.ds(0, n - 1)], filter_sems.at[0], filter_sems.at[1]).wait_send()
        waiter(lag_out.at[pl.ds(0, pairs - 1)], lag_sems.at[0], lag_sems.at[1]).wait_send()
        waiter(lag_in.at[pl.ds(0, n - 1)], lag_sems.at[0], lag_sems.at[1]).wait_recv()

    @pl.when(me >= pairs)
    def _():
        lag_in[...] = jnp.zeros_like(lag_in)
        waiter(lag_out, lag_sems.at[0], lag_sems.at[1]).wait_send()

    def finish(piece, _):
        waiter(
            recv.at[pl.ds(0, n - 1), chosen(piece)], out_sems.at[piece], in_sems.at[piece]
        ).wait_send()
        waiter(
            back_out.at[pl.ds(0, n - 1), chosen(piece)], back_out_sems.at[piece],
            back_in_sems.at[piece],
        ).wait()
        return 0

    lax.fori_loop(0, pieces, finish, 0)
    channels = query.shape[1]
    width = channels // repeats
    for half in range(2):
        for start in range(0, channels, HALF):
            at = (slice(half * HALF, (half + 1) * HALF), slice(start, start + HALF))
            row = start % width * GROUP + half * 4 + start // width
            back = back_in[pl.ds(row, HALF, stride=GROUP)].T
            grad_query[at] = (back * key[at].astype(jnp.float32)).astype(jnp.bfloat16)
            grad_key[at] = (back * query[at].astype(jnp.float32)).astype(jnp.bfloat16)


def convolve(genomes, query, key, value, grad, filters):
    n, own = filters.shape[:2]
    pairs = n // 2
    pieces = own // PART
    rows = GROUP * n
    padded = rows + 4 * n
    repeats = query.shape[1] // (n * own)
    signals = (n, own, 2, GROUP, HALF)
    vmem = pl.BlockSpec(memory_space=pltpu.VMEM)
    flops = own * 2 * pairs * 2 * rows * 256 * (256 + 128 + 192)
    return pl.pallas_call(
        functools.partial(fused_kernel, repeats),
        in_specs=[pl.BlockSpec(memory_space=pltpu.SMEM)] + [vmem] * 5,
        out_specs=[vmem] * 3,
        out_shape=[
            jax.ShapeDtypeStruct(query.shape, jnp.bfloat16),
            jax.ShapeDtypeStruct(query.shape, jnp.bfloat16),
            jax.ShapeDtypeStruct((n, 2, own, 1, HALF), jnp.float32),
        ],
        scratch_shapes=[
            pltpu.VMEM((n * own * 2 * GROUP, HALF), jnp.float32),
            pltpu.VMEM(signals, jnp.float32),
            pltpu.VMEM((n * own * GROUP, HALF), jnp.float32),
            pltpu.VMEM((pairs, own, 2, 1, HALF), jnp.float32),
            pltpu.VMEM((n, own, GROUP, HALF), jnp.float32),
            pltpu.VMEM((pairs, 2, own, 1, HALF), jnp.float32),
            pltpu.VMEM((n, rows, HALF), jnp.bfloat16),
            pltpu.VMEM((rows + 16, HALF), jnp.float32),
            pltpu.VMEM((4, padded, HALF), jnp.bfloat16),
            pltpu.VMEM((4, padded, HALF), jnp.bfloat16),
            pltpu.VMEM((pairs // UNROLL, 256 * UNROLL, 256), jnp.bfloat16),
            pltpu.VMEM((2 * rows, 256), jnp.float32),
            pltpu.VMEM((2 * pairs + 1, GROUP, HALF), jnp.float32),
            pltpu.VMEM((2 * pairs, GROUP, HALF), jnp.float32),
            pltpu.SemaphoreType.DMA((2,)),
            pltpu.SemaphoreType.DMA((2,)),
            pltpu.SemaphoreType.DMA((pieces,)),
            pltpu.SemaphoreType.DMA((pieces,)),
            pltpu.SemaphoreType.DMA((pieces,)),
            pltpu.SemaphoreType.DMA((pieces,)),
        ],
        compiler_params=pltpu.CompilerParams(
            collective_id=0, has_side_effects=True, vmem_limit_bytes=52 * 1024 * 1024
        ),
        cost_estimate=pl.CostEstimate(
            flops=flops, bytes_accessed=5 * query.size * 2, transcendentals=0
        ),
    )(genomes, query, key, value, grad, filters)


def local(query_branch, key_branch, value_branch, grad_output, conv_output, filters, genome_blocks):
    rows, channels = query_branch.shape
    width = filters.shape[1]
    blocks = lax.axis_size("ctx")
    own = width // blocks
    grad_value = (grad_output.astype(jnp.float32) * conv_output.astype(jnp.float32)).astype(
        jnp.bfloat16
    )
    filter_parts = filters.reshape(2, HALF, blocks, own)[:, ::-1].transpose(2, 3, 0, 1)
    grad_query, grad_key, lag = convolve(
        genome_blocks, query_branch, key_branch, value_branch, grad_output,
        filter_parts[:, :, :, None],
    )
    lag = lag[:, :, :, 0].transpose(1, 3, 0, 2).reshape(rows, width)
    scaled = lag * (rows * blocks) ** (-0.5)
    grad_filters = lax.psum_scatter(scaled, "ch", scatter_dimension=1, tiled=True)
    return (grad_query, grad_key, grad_value, grad_filters)


def solution(mesh):
    in_specs = (
        P("ctx", "ch"),
        P("ctx", "ch"),
        P("ctx", "ch"),
        P("ctx", "ch"),
        P("ctx", "ch"),
        P("ctx", None),
        P(),
    )
    out_specs = (P("ctx", "ch"), P("ctx", "ch"), P("ctx", "ch"), P("ctx", "ch"))
    return jax.shard_map(local, mesh=mesh, in_specs=in_specs, out_specs=out_specs, check_vma=False)
```

```python
import functools

import jax
import jax.numpy as jnp
from jax import lax
from jax.experimental import pallas as pl
from jax.experimental.pallas import tpu as pltpu
from jax.sharding import PartitionSpec as P

HALF = 128
GROUP = 8
PART = 4
UNROLL = 4
STRIDE = 13
EARLY = 1
NT = (((1,), (1,)), ((), ()))


def split_bf16(x):
    high = x.astype(jnp.bfloat16)
    low = (x - high.astype(jnp.float32)).astype(jnp.bfloat16)
    return high, low


def make_masks(genomes, masks):
    lags, rows = masks.shape[:2]
    row = lax.broadcasted_iota(jnp.int32, (rows, HALF), 0)

    def owner(place):
        block = lax.shift_right_logical(place, 3)
        found = jnp.zeros((rows, HALF), jnp.int32)
        end = 0
        for g in range(genomes.shape[0]):
            end = end + genomes[g]
            found = found + jnp.where(block >= end, 1, 0)
        return found

    own = owner(row)

    def one(lag, _):
        same = owner(row + 4 * lag) == own
        masks[lag] = jnp.where(same, 1.0, 0.0).astype(jnp.bfloat16)
        return 0

    lax.fori_loop(0, lags, one, 0)


def conv_one(
    f, masks, recv, filter_in, back_out, lag_out,
    base, shift_high, shift_low, weights, accum, low_sum, high_sum,
):
    n = recv.shape[0]
    rows = GROUP * n
    pairs = filter_in.shape[0]
    lane = lax.broadcasted_iota(jnp.int32, (GROUP, HALF), 1)
    place = lax.broadcasted_iota(jnp.int32, (GROUP, HALF), 0)

    base[:rows] = recv[:, f, 0].reshape(rows, HALF)
    for move in range(4):
        high, low = split_bf16(base[4 * move:4 * move + rows])
        shift_high[move, :rows] = high
        shift_low[move, :rows] = low

    def build(c, before):
        for pair in range(UNROLL):
            for side in range(2):
                row = filter_in[c * UNROLL + pair, f, side]
                first = pltpu.roll(
                    jnp.broadcast_to(row, (GROUP, HALF)), 1, 1, stride=1, stride_axis=0
                )
                turned = [first] + [
                    pltpu.roll(first, GROUP * p, 1) for p in range(1, HALF // GROUP)
                ]
                tile = jnp.concatenate(
                    [
                        jnp.where(lane <= place + GROUP * p, turned[p], before[p])
                        for p in range(HALF // GROUP)
                    ],
                    axis=0,
                )
                high, low = split_bf16(tile)
                at = pair * 2 * HALF + side * HALF
                weights[c, at:at + HALF, :HALF] = high
                weights[c, at:at + HALF, HALF:] = low
                before = turned
        return before

    lax.fori_loop(
        0, pairs // UNROLL, build, [jnp.zeros((GROUP, HALF), jnp.float32)] * (HALF // GROUP)
    )

    swap = (
        lax.broadcasted_iota(jnp.int32, (HALF, HALF), 1)
        + lax.broadcasted_iota(jnp.int32, (HALF, HALF), 0)
        == HALF - 1
    ).astype(jnp.bfloat16)
    gated_high, gated_low = split_bf16(recv[:, f, 1].reshape(rows, HALF))
    turned_high = lax.dot_general(
        swap, gated_high, NT, preferred_element_type=jnp.float32
    ).astype(jnp.bfloat16)
    turned_low = lax.dot_general(
        swap, gated_low, NT, preferred_element_type=jnp.float32
    ).astype(jnp.bfloat16)
    turned_both = jnp.concatenate([turned_high, turned_low], axis=0)

    accum[...] = jnp.zeros_like(accum)

    def lag_group(c, _):
        highs, lows = [], []
        for e in range(2 * UNROLL):
            lag = 2 * UNROLL * c + e
            window = pl.ds(pl.multiple_of((2 * UNROLL * c + e - e % 4) * 4, 16), rows)
            mask = masks[lag]
            highs.append(shift_high[e % 4, window] * mask)
            lows.append(shift_low[e % 4, window] * mask)
        high = jnp.concatenate(highs, axis=1)
        low = jnp.concatenate(lows, axis=1)
        accum[...] += jnp.dot(
            jnp.concatenate([high, low], axis=0), weights[c], preferred_element_type=jnp.float32
        )
        both = jnp.dot(turned_both, high, preferred_element_type=jnp.float32)
        outer = (
            both[:HALF] + both[HALF:] + jnp.dot(turned_high, low, preferred_element_type=jnp.float32)
        )
        for side in range(2 * UNROLL):
            here = jnp.zeros((GROUP, HALF), jnp.float32)
            prior = jnp.zeros((GROUP, HALF), jnp.float32)
            for p in range(HALF // GROUP):
                part = outer[GROUP * p:GROUP * p + GROUP, side * HALF:(side + 1) * HALF]
                part = pltpu.roll(part, GROUP * p + 1, 1)
                inside = lane <= GROUP * p
                here = here + jnp.where(inside, part, 0.0)
                prior = prior + jnp.where(inside, 0.0, part)
            here = pltpu.roll(here, 0, 1, stride=1, stride_axis=0)
            prior = pltpu.roll(prior, 0, 1, stride=1, stride_axis=0)
            wrapped = lane < place
            high_sum[2 * UNROLL * c + side] = here + jnp.where(wrapped, prior, 0.0)
            low_sum[2 * UNROLL * c + side] = jnp.where(wrapped, 0.0, prior)
        return 0

    lax.fori_loop(0, pairs // UNROLL, lag_group, 0)
    total = (
        accum[:rows, :HALF] + accum[:rows, HALF:] + accum[rows:, :HALF] + accum[rows:, HALF:]
    )
    back_out[:, f] = total.reshape(n, GROUP, HALF)
    lags = jnp.sum(high_sum[...] + low_sum[1:], axis=1, keepdims=True)
    lag_out[:, :, f] = lags.reshape(pairs, 2, 1, HALF)


def spread_product(first, second, sig, send_rows, repeats):
    channels = first.shape[1]
    width = channels // repeats
    for half in range(2):
        for start in range(0, channels, HALF):
            at = (slice(half * HALF, (half + 1) * HALF), slice(start, start + HALF))
            product = first[at].astype(jnp.float32) * second[at].astype(jnp.float32)
            turn, column = start // width, start % width
            row = column * 2 * GROUP + sig * GROUP + half * 4 + turn
            send_rows[pl.ds(row, HALF, stride=2 * GROUP)] = product.T


def fused_kernel(
    repeats, genomes, query, key, value, grad, filter_send,
    grad_query, grad_key, lag_in,
    send, recv, back_in, filter_in, back_out, lag_out,
    masks, base, shift_high, shift_low, weights, accum, low_sum, high_sum,
    filter_sems, lag_sems, out_sems, in_sems, back_out_sems, back_in_sems,
):
    n, own = filter_send.shape[:2]
    pairs = filter_in.shape[0]
    pieces = own // PART
    me = lax.axis_index("ctx")

    def partner(i):
        return lax.rem(me + STRIDE * i, n)

    def copy(source, target, send_sem, recv_sem, device):
        return pltpu.make_async_remote_copy(
            src_ref=source, dst_ref=target, send_sem=send_sem, recv_sem=recv_sem,
            device_id={"ctx": device}, device_id_type=pl.DeviceIdType.MESH,
        )

    def each_partner(act):
        def step(i, _):
            act(partner(i))
            return 0

        lax.fori_loop(1, n, step, 0)

    def chosen(piece):
        return pl.ds(piece * PART, PART)

    def sent(other, piece):
        count = PART * 2 * GROUP
        start = pl.multiple_of(other * (own * 2 * GROUP) + piece * count, count)
        return send.at[pl.ds(start, count)].reshape(PART, 2, GROUP, HALF)

    def returned(piece):
        count = PART * GROUP
        start = pl.multiple_of(me * (own * GROUP) + piece * count, count)
        return back_in.at[pl.ds(start, count)].reshape(PART, GROUP, HALF)

    def waiter(ref, send_sem, recv_sem):
        return copy(ref, ref, send_sem, recv_sem, partner(1))

    barrier = pltpu.get_barrier_semaphore()
    each_partner(
        lambda other: pl.semaphore_signal(
            barrier, inc=1, device_id={"ctx": other}, device_id_type=pl.DeviceIdType.MESH
        )
    )
    pl.semaphore_wait(barrier, n - 1)

    @pl.when(me < pairs)
    def _():
        each_partner(
            lambda other: copy(
                filter_send.at[other], filter_in.at[me], filter_sems.at[0], filter_sems.at[1], other
            ).start()
        )

    if repeats < 4:
        send[...] = jnp.zeros_like(send)

    def send_half(sig):
        def one(piece, _):
            each_partner(
                lambda other: copy(
                    sent(other, piece).at[:, sig], recv.at[me, chosen(piece), sig],
                    out_sems.at[piece], in_sems.at[piece], other,
                ).start()
            )
            return 0

        lax.fori_loop(0, EARLY, one, 0)

    def send_piece(piece, _):
        each_partner(
            lambda other: copy(
                sent(other, piece), recv.at[me, chosen(piece)],
                out_sems.at[piece], in_sems.at[piece], other,
            ).start()
        )
        return 0

    spread_product(grad, value, 0, send, repeats)
    send_half(0)
    spread_product(query, key, 1, send, repeats)
    send_half(1)
    lax.fori_loop(EARLY, pieces, send_piece, 0)

    mine = send[pl.ds(pl.multiple_of(me * (own * 2 * GROUP), 16), own * 2 * GROUP)]
    recv[me] = mine.reshape(own, 2, GROUP, HALF)
    make_masks(genomes, masks)
    base[...] = jnp.zeros_like(base)
    shift_high[...] = jnp.zeros_like(shift_high)
    shift_low[...] = jnp.zeros_like(shift_low)
    low_sum[2 * pairs] = jnp.zeros((GROUP, HALF), jnp.float32)

    @pl.when(me < pairs)
    def _():
        filter_in[me] = filter_send[me]
        waiter(filter_in.at[pl.ds(0, pairs - 1)], filter_sems.at[0], filter_sems.at[1]).wait_recv()

    @pl.when(me >= pairs)
    def _():
        waiter(filter_in, filter_sems.at[0], filter_sems.at[1]).wait_recv()

    def work(piece, _):
        waiter(
            recv.at[pl.ds(0, n - 1), chosen(piece)], out_sems.at[piece], in_sems.at[piece]
        ).wait_recv()

        def one(i, _):
            conv_one(
                piece * PART + i, masks, recv, filter_in, back_out, lag_out,
                base, shift_high, shift_low, weights, accum, low_sum, high_sum,
            )
            return 0

        lax.fori_loop(0, PART, one, 0)
        each_partner(
            lambda other: copy(
                back_out.at[other, chosen(piece)], returned(piece),
                back_out_sems.at[piece], back_in_sems.at[piece], other,
            ).start()
        )
        start = pl.multiple_of(me * (own * GROUP) + piece * (PART * GROUP), PART * GROUP)
        back_in[pl.ds(start, PART * GROUP)] = back_out[me, chosen(piece)].reshape(
            PART * GROUP, HALF
        )

        def send_lags(other, _):
            @pl.when(other != me)
            def _():
                copy(
                    lag_out.at[other, :, chosen(piece)], lag_in.at[me, :, chosen(piece)],
                    lag_sems.at[0], lag_sems.at[1], other,
                ).start()

            return 0

        lax.fori_loop(0, pairs, send_lags, 0)
        return 0

    lax.fori_loop(0, pieces, work, 0)

    @pl.when(me < pairs)
    def _():
        lag_in[me] = lag_out[me]
        waiter(filter_send.at[pl.ds(0, n - 1)], filter_sems.at[0], filter_sems.at[1]).wait_send()
        waiter(lag_out.at[pl.ds(0, pairs - 1)], lag_sems.at[0], lag_sems.at[1]).wait_send()
        waiter(lag_in.at[pl.ds(0, n - 1)], lag_sems.at[0], lag_sems.at[1]).wait_recv()

    @pl.when(me >= pairs)
    def _():
        lag_in[...] = jnp.zeros_like(lag_in)
        waiter(lag_out, lag_sems.at[0], lag_sems.at[1]).wait_send()

    def finish(piece, _):
        waiter(
            recv.at[pl.ds(0, n - 1), chosen(piece)], out_sems.at[piece], in_sems.at[piece]
        ).wait_send()
        waiter(
            back_out.at[pl.ds(0, n - 1), chosen(piece)], back_out_sems.at[piece],
            back_in_sems.at[piece],
        ).wait()
        return 0

    lax.fori_loop(0, pieces, finish, 0)
    channels = query.shape[1]
    width = channels // repeats
    for half in range(2):
        for start in range(0, channels, HALF):
            at = (slice(half * HALF, (half + 1) * HALF), slice(start, start + HALF))
            row = start % width * GROUP + half * 4 + start // width
            back = back_in[pl.ds(row, HALF, stride=GROUP)].T
            grad_query[at] = (back * key[at].astype(jnp.float32)).astype(jnp.bfloat16)
            grad_key[at] = (back * query[at].astype(jnp.float32)).astype(jnp.bfloat16)


def convolve(genomes, query, key, value, grad, filters):
    n, own = filters.shape[:2]
    pairs = n // 2
    pieces = own // PART
    rows = GROUP * n
    padded = rows + 4 * n
    repeats = query.shape[1] // (n * own)
    signals = (n, own, 2, GROUP, HALF)
    vmem = pl.BlockSpec(memory_space=pltpu.VMEM)
    flops = own * 2 * pairs * 2 * rows * 256 * (256 + 128 + 192)
    return pl.pallas_call(
        functools.partial(fused_kernel, repeats),
        in_specs=[pl.BlockSpec(memory_space=pltpu.SMEM)] + [vmem] * 5,
        out_specs=[vmem] * 3,
        out_shape=[
            jax.ShapeDtypeStruct(query.shape, jnp.bfloat16),
            jax.ShapeDtypeStruct(query.shape, jnp.bfloat16),
            jax.ShapeDtypeStruct((n, 2, own, 1, HALF), jnp.float32),
        ],
        scratch_shapes=[
            pltpu.VMEM((n * own * 2 * GROUP, HALF), jnp.float32),
            pltpu.VMEM(signals, jnp.float32),
            pltpu.VMEM((n * own * GROUP, HALF), jnp.float32),
            pltpu.VMEM((pairs, own, 2, 1, HALF), jnp.float32),
            pltpu.VMEM((n, own, GROUP, HALF), jnp.float32),
            pltpu.VMEM((pairs, 2, own, 1, HALF), jnp.float32),
            pltpu.VMEM((n, rows, HALF), jnp.bfloat16),
            pltpu.VMEM((rows + 16, HALF), jnp.float32),
            pltpu.VMEM((4, padded, HALF), jnp.bfloat16),
            pltpu.VMEM((4, padded, HALF), jnp.bfloat16),
            pltpu.VMEM((pairs // UNROLL, 256 * UNROLL, 256), jnp.bfloat16),
            pltpu.VMEM((2 * rows, 256), jnp.float32),
            pltpu.VMEM((2 * pairs + 1, GROUP, HALF), jnp.float32),
            pltpu.VMEM((2 * pairs, GROUP, HALF), jnp.float32),
            pltpu.SemaphoreType.DMA((2,)),
            pltpu.SemaphoreType.DMA((2,)),
            pltpu.SemaphoreType.DMA((pieces,)),
            pltpu.SemaphoreType.DMA((pieces,)),
            pltpu.SemaphoreType.DMA((pieces,)),
            pltpu.SemaphoreType.DMA((pieces,)),
        ],
        compiler_params=pltpu.CompilerParams(
            collective_id=0, has_side_effects=True, vmem_limit_bytes=52 * 1024 * 1024
        ),
        cost_estimate=pl.CostEstimate(
            flops=flops, bytes_accessed=5 * query.size * 2, transcendentals=0
        ),
    )(genomes, query, key, value, grad, filters)


def local(query_branch, key_branch, value_branch, grad_output, conv_output, filters, genome_blocks):
    rows, channels = query_branch.shape
    width = filters.shape[1]
    blocks = lax.axis_size("ctx")
    own = width // blocks
    grad_value = (grad_output.astype(jnp.float32) * conv_output.astype(jnp.float32)).astype(
        jnp.bfloat16
    )
    filter_parts = filters.reshape(2, HALF, blocks, own)[:, ::-1].transpose(2, 3, 0, 1)
    grad_query, grad_key, lag = convolve(
        genome_blocks, query_branch, key_branch, value_branch, grad_output,
        filter_parts[:, :, :, None],
    )
    lag = lag[:, :, :, 0].transpose(1, 3, 0, 2).reshape(rows, width)
    scaled = lag * (rows * blocks) ** (-0.5)
    grad_filters = lax.psum_scatter(scaled, "ch", scatter_dimension=1, tiled=True)
    return (grad_query, grad_key, grad_value, grad_filters)


def solution(mesh):
    in_specs = (
        P("ctx", "ch"),
        P("ctx", "ch"),
        P("ctx", "ch"),
        P("ctx", "ch"),
        P("ctx", "ch"),
        P("ctx", None),
        P(),
    )
    out_specs = (P("ctx", "ch"), P("ctx", "ch"), P("ctx", "ch"), P("ctx", "ch"))
    return jax.shard_map(local, mesh=mesh, in_specs=in_specs, out_specs=out_specs, check_vma=False)
```
